256 devices in a mesh: wide: 32 (over z, x), narrow: 8 (over y, core).
Axes of the slice: x: 4, y: 4, z: 8, core: 2. Of those that a mesh axis runs over, the one named last changes fastest.
Arguments:
- row_codes: bfloat16 [131072, 512], P('wide'), may hold values from -127 to 127
- row_scales: float32 [131072], P('wide'), may hold values from 0.004 to 0.04
- row_biases: float32 [131072], P('wide'), may hold values from -0.32 to 0.32, as said below
- cluster_ids: int32 [131072], P('wide'), may hold values from 0 to 499, as said below
- order_index: int32 [131072], P('wide'), may hold values from 0 to 131071, each once
Outputs:
- nearest_sim: float32 [131072], P('wide')
The draws below stay inside these ranges and needn't reach their ends.
Inputs may be any that keep to these rules, and one draw needn't show every extreme that they name: `cluster_ids`: cluster c belongs to owner c % 32. At most 256 rows of one index of wide belong to clusters of one owner, and in every draw one owner receives exactly 256 rows from every index of wide. `row_biases`: the absolute value of each row's offset is at most 8 times that row's scale.
All inputs are finite; a program needn't handle non-finite values.
Results may differ from the reference program's by a relative error of at most 0.0015.
Values may be sent and summed in bfloat16 or wider, within the bound.
No kernel may reach another device: no remote copies, remote signals or barrier semaphores. Data moves between devices by JAX's collectives and lax.ppermute only.
A program may use at most 64 MiB of HBM per device.

```python
import jax
import jax.numpy as jnp
from jax import lax

EMBED = 512
CLUSTERS = 500
ROWS_DEV = 4096
CAP = 256
ROWS = 131072
N_WIDE = 32


def cluster_layout(key):
    hot_owner = jax.random.randint(jax.random.fold_in(key, 11), (), 0, N_WIDE)
    positions = jnp.arange(ROWS_DEV, dtype=jnp.int32)
    spread_pos = jnp.maximum(positions - CAP, 0) % (N_WIDE - 1)
    targets = jnp.where(positions < CAP, hot_owner, (hot_owner + 1 + spread_pos) % N_WIDE)
    shuffle_keys = jax.random.split(jax.random.fold_in(key, 12), N_WIDE)
    shuffled = jax.vmap(lambda sub_key: targets[jax.random.permutation(sub_key, ROWS_DEV)])(shuffle_keys)
    counts = (CLUSTERS - 1 - shuffled) // N_WIDE + 1
    first_pick = jax.random.randint(jax.random.fold_in(key, 13), shuffled.shape, 0, counts)
    second_pick = jax.random.randint(jax.random.fold_in(key, 14), shuffled.shape, 0, counts)
    chosen = shuffled + N_WIDE * jnp.minimum(first_pick, second_pick)
    return chosen.reshape(ROWS_DEV * N_WIDE).astype(jnp.int32)


def scale_layout(key):
    low_log = jnp.log(jnp.float32(0.004))
    high_log = jnp.log(jnp.float32(0.04))
    drawn = jax.random.uniform(jax.random.fold_in(key, 21), (ROWS_DEV * N_WIDE,), jnp.float32, 0.0, 1.0)
    return jnp.exp(low_log + (high_log - low_log) * drawn)


def draw_row_scales(key, part):
    scales = scale_layout(key)
    return scales


def draw_row_biases(key, part):
    scales = scale_layout(key)
    key = jax.random.fold_in(key, 32)
    offsets = jax.random.uniform(key, (ROWS_DEV * N_WIDE,), jnp.float32, -8.0, 8.0)
    return scales * offsets


def draw_cluster_ids(key, part):
    return cluster_layout(key)


def draw_row_codes(key, part):
    clusters = cluster_layout(key)
    key = jax.random.fold_in(key, 5)
    total_rows = ROWS_DEV * N_WIDE
    centers = jax.random.normal(jax.random.fold_in(key, 1), (CLUSTERS, EMBED), jnp.float32)
    noise_part = jax.random.normal(jax.random.fold_in(key, 2), (total_rows, EMBED), jnp.float32)
    row_gain = jnp.ones((total_rows, 1), jnp.float32)
    base_rows = noise_part + 0.6 * centers[clusters]
    ordering = jnp.argsort(clusters, stable=True).astype(jnp.int32)
    sorted_cluster = clusters[ordering]
    seg_first = jnp.searchsorted(sorted_cluster, sorted_cluster, side='left').astype(jnp.int32)
    seg_after = jnp.searchsorted(sorted_cluster, sorted_cluster, side='right').astype(jnp.int32)
    positions = jnp.arange(total_rows, dtype=jnp.int32)
    jump_sizes = jax.random.randint(jax.random.fold_in(key, 3), (total_rows,), 1, 200)
    partner_place = seg_first + (positions - seg_first + jump_sizes) % (seg_after - seg_first)
    partner = jnp.zeros((total_rows,), jnp.int32).at[ordering].set(ordering[partner_place])
    duplicate = (jax.random.randint(jax.random.fold_in(key, 4), (total_rows,), 0, 3) == 0).astype(jnp.float32)
    strength = jnp.exp(jax.random.uniform(jax.random.fold_in(key, 7), (total_rows,), jnp.float32, 0.0, 1.4))
    embedded = base_rows + (duplicate * strength)[:, None] * base_rows[partner]
    return jnp.clip(18.0 * row_gain * embedded, -127.0, 127.0).astype(jnp.bfloat16)


def setup_inputs(seed: int = 0) -> dict:
    keys = jax.random.split(jax.random.key(seed), 6)
    row_codes = draw_row_codes(jax.random.fold_in(keys[5], 71), 0)
    row_scales = draw_row_scales(jax.random.fold_in(keys[5], 71), 0)
    row_biases = draw_row_biases(jax.random.fold_in(keys[5], 71), 0)
    cluster_ids = draw_cluster_ids(jax.random.fold_in(keys[5], 71), 0)
    order_index = jax.random.permutation(keys[4], ROWS).astype(jnp.int32)
    return dict(row_codes=row_codes, row_scales=row_scales, row_biases=row_biases, cluster_ids=cluster_ids, order_index=order_index)


epsilon = 1e-06

def reference(row_codes, row_scales, row_biases, cluster_ids, order_index):
    values = row_codes.astype(jnp.float32) * row_scales[:, None] + row_biases[:, None]
    unit_rows = (values * lax.rsqrt(lax.optimization_barrier(jnp.mean(values * values, axis=1, keepdims=True)) + epsilon)).astype(jnp.bfloat16)
    row_total = cluster_ids.shape[0]
    sort_key = cluster_ids * row_total + order_index
    ordering = jnp.argsort(sort_key).astype(jnp.int32)
    sorted_rows = unit_rows[ordering]
    sorted_cluster = cluster_ids[ordering]
    sorted_order = order_index[ordering]
    cluster_first = jnp.searchsorted(sorted_cluster, sorted_cluster, side='left').astype(jnp.int32)
    block_rows = min(512, row_total)
    blocks = row_total // block_rows

    def one_block(block_index):
        begin_row = (block_index * block_rows).astype(jnp.int32)
        queries = lax.dynamic_slice_in_dim(sorted_rows, begin_row, block_rows, 0)
        query_cluster = lax.dynamic_slice_in_dim(sorted_cluster, begin_row, block_rows, 0)
        query_order = lax.dynamic_slice_in_dim(sorted_order, begin_row, block_rows, 0)
        lowest = lax.dynamic_slice_in_dim(cluster_first, begin_row, 1, 0)[0] // block_rows

        def visit_block(key_index, running):
            key_begin = (key_index * block_rows).astype(jnp.int32)
            key_rows = lax.dynamic_slice_in_dim(sorted_rows, key_begin, block_rows, 0)
            key_cluster = lax.dynamic_slice_in_dim(sorted_cluster, key_begin, block_rows, 0)
            key_order = lax.dynamic_slice_in_dim(sorted_order, key_begin, block_rows, 0)
            scores = jnp.dot(queries, key_rows.T, preferred_element_type=jnp.float32) / EMBED
            allowed = (query_cluster[:, None] == key_cluster[None, :]) & (key_order[None, :] < query_order[:, None])
            return jnp.maximum(running, lax.optimization_barrier(jnp.max(jnp.where(allowed, scores, -1.0), axis=1)))
        start_best = jnp.full((block_rows,), -1.0, jnp.float32)
        return lax.fori_loop(lowest, block_index + 1, visit_block, start_best)
    best_sorted = lax.map(one_block, jnp.arange(blocks, dtype=jnp.int32)).reshape(row_total)
    return jnp.zeros((row_total,), jnp.float32).at[ordering].set(best_sorted)
```

```python
import functools

import jax
import jax.numpy as jnp
from jax import lax
from jax.experimental import pallas as pl
from jax.experimental.pallas import tpu as pltpu
from jax.sharding import PartitionSpec as P

epsilon = 1e-06

BLOCK = 56
SLOTS = BLOCK - 1
LANES = 128
CHUNK = 256
ORDER_SPAN = 131072
VMEM_LIMIT = 48 * 1024 * 1024


def iota(shape, axis):
    return lax.broadcasted_iota(jnp.int32, shape, axis)


def dot(left, right, left_axis, right_axis):
    return lax.dot_general(
        left, right, (((left_axis,), (right_axis,)), ((), ())), preferred_element_type=jnp.float32
    )


def strictly_before():
    return (iota((CHUNK, CHUNK), 0) < iota((CHUNK, CHUNK), 1)).astype(jnp.bfloat16)


def chunk_of(ref, index):
    return jnp.concatenate([ref[2 * index : 2 * index + 1, :], ref[2 * index + 1 : 2 * index + 2, :]], axis=1)


def owner_and_peer(clusters, owners, peers):
    owner = clusters & (owners - 1)
    place = clusters >> (owners.bit_length() - 1)
    peer = jnp.minimum(place, 2 * peers - 1 - place)
    return owner, place, peer


def pack_kernel(
    owners, peers, cluster_ref, order_ref, scale_ref, bias_ref, codes_hbm, out_ref,
    codes_half, codes_full, slots_full, table_vmem, table_smem, code_sems, table_sem,
):
    local_rows = codes_hbm.shape[0]
    me_wide = lax.axis_index("wide")
    me_narrow = lax.axis_index("narrow")
    pieces = code_sems.shape[0]
    piece = local_rows // pieces
    copies = [
        pltpu.make_async_copy(
            codes_hbm.at[pl.ds(n * piece, piece)], codes_half.at[pl.ds(n * piece, piece)], code_sems.at[n]
        )
        for n in range(pieces)
    ]
    for copy in copies:
        copy.start()

    before = strictly_before()
    count = jnp.zeros((owners, 1), jnp.float32)
    meta = jnp.zeros((owners, 3 * LANES), jnp.float32)
    table = jnp.zeros((136, owners), jnp.float32)
    for n in range(local_rows // CHUNK):
        clusters = chunk_of(cluster_ref, n)
        orders = chunk_of(order_ref, n)
        owner, place, peer = owner_and_peer(clusters, owners, peers)
        owner = jnp.where(peer == me_narrow, owner, -1)
        mine = iota((owners, CHUNK), 0) == owner
        one_hot = jnp.where(mine, 1.0, 0.0)
        one_hot_half = one_hot.astype(jnp.bfloat16)
        earlier = dot(one_hot_half, before, 1, 0) + count
        rank = jnp.sum(jnp.where(mine, earlier, 0.0), axis=0, keepdims=True).astype(jnp.int32)
        count = count + jnp.sum(one_hot, axis=1, keepdims=True)
        lane = (me_wide * BLOCK + rank) & (LANES - 1)
        key = place * ORDER_SPAN + orders + 1
        row = n * CHUNK + iota((1, CHUNK), 1)
        at_lane = iota((LANES, CHUNK), 0) == lane
        at_rank = iota((64, CHUNK), 0) == rank

        def spread(mask, value):
            return jnp.where(mask, value.astype(jnp.float32), 0.0)

        meta_parts = jnp.concatenate(
            [spread(at_lane, key >> 16), spread(at_lane, (key >> 8) & 255), spread(at_lane, key & 255)], axis=0
        ).astype(jnp.bfloat16)
        table_parts = jnp.concatenate(
            [spread(at_rank, row >> 6), spread(at_rank, row & 63), jnp.ones((8, CHUNK), jnp.float32)], axis=0
        ).astype(jnp.bfloat16)
        meta = meta + dot(one_hot_half, meta_parts, 1, 1)
        table = table + dot(table_parts, one_hot_half, 1, 1)
    rows_at = table[0:64] * 64.0 + table[64:128]
    table_vmem[...] = jnp.concatenate(
        [
            jnp.concatenate([rows_at, table[128:136]], axis=0),
            jnp.zeros((72, LANES - owners), jnp.float32),
        ],
        axis=1,
    ).astype(jnp.int32)
    table_copy = pltpu.make_async_copy(table_vmem, table_smem, table_sem)
    table_copy.start()
    over = jnp.where(jnp.max(count) > SLOTS, 1.0, 0.0)
    meta = jnp.concatenate([meta, jnp.full((owners, LANES), over, jnp.float32)], axis=1)

    slots_full[...] = jnp.zeros_like(slots_full)
    for n, copy in enumerate(copies):
        copy.wait()
        codes_full[n * piece : (n + 1) * piece, :] = codes_half[n * piece : (n + 1) * piece, :].astype(jnp.float32)
    table_copy.wait()

    def one_owner(owner, carry):
        used = jnp.minimum(table_smem[64, owner], SLOTS)

        def eight_rows(group, carry):
            for n in range(8):
                slot = group * 8 + n
                row = table_smem[slot, owner]
                slots_full[pl.ds(owner * BLOCK + slot, 1), :] = (
                    codes_full[pl.ds(row, 1), :] * scale_ref[row] + bias_ref[row]
                )
            return carry

        return lax.fori_loop(0, (used + 7) // 8, eight_rows, carry)

    lax.fori_loop(0, owners, one_owner, 0)

    pair = 2 * BLOCK
    for n in range(owners // 2):
        values = slots_full[n * pair : (n + 1) * pair, :]
        mean_square = jnp.mean(values * values, axis=1, keepdims=True)
        unit = values * lax.rsqrt(mean_square + epsilon)
        place = iota((pair, 1), 0)
        unit = jnp.where(place == SLOTS, meta[2 * n : 2 * n + 1], unit)
        unit = jnp.where(place == BLOCK + SLOTS, meta[2 * n + 1 : 2 * n + 2], unit)
        out_ref[n * pair : (n + 1) * pair, :] = unit.astype(jnp.bfloat16)


def pack(row_codes, row_scales, row_biases, cluster_ids, order_index, owners, peers):
    local_rows, width = row_codes.shape
    whole = pl.BlockSpec(memory_space=pltpu.VMEM)
    scalars = pl.BlockSpec(memory_space=pltpu.SMEM)
    pieces = 8
    return pl.pallas_call(
        functools.partial(pack_kernel, owners, peers),
        out_shape=jax.ShapeDtypeStruct((owners * BLOCK, width), jnp.bfloat16),
        in_specs=[whole, whole, scalars, scalars, pl.BlockSpec(memory_space=pl.ANY)],
        out_specs=whole,
        scratch_shapes=[
            pltpu.VMEM((local_rows, width), jnp.bfloat16),
            pltpu.VMEM((local_rows, width), jnp.float32),
            pltpu.VMEM((owners * BLOCK, width), jnp.float32),
            pltpu.VMEM((72, LANES), jnp.int32),
            pltpu.SMEM((72, LANES), jnp.int32),
            pltpu.SemaphoreType.DMA((pieces,)),
            pltpu.SemaphoreType.DMA,
        ],
        compiler_params=pltpu.CompilerParams(vmem_limit_bytes=VMEM_LIMIT),
        name="pack",
    )(
        cluster_ids.reshape(-1, LANES), order_index.reshape(-1, LANES), row_scales, row_biases, row_codes,
    )


def place_kernel(owners, peers, cluster_ref, group_ref, lane_ref):
    me_wide = lax.axis_index("wide")
    groups = owners * peers
    before = strictly_before()
    count = jnp.zeros((groups, 1), jnp.float32)
    for n in range(cluster_ref.shape[0] // 2):
        owner, _, peer = owner_and_peer(chunk_of(cluster_ref, n), owners, peers)
        group = peer * owners + owner
        mine = iota((groups, CHUNK), 0) == group
        one_hot = jnp.where(mine, 1.0, 0.0)
        earlier = dot(one_hot.astype(jnp.bfloat16), before, 1, 0) + count
        rank = jnp.sum(jnp.where(mine, earlier, 0.0), axis=0, keepdims=True).astype(jnp.int32)
        count = count + jnp.sum(one_hot, axis=1, keepdims=True)
        lane = (me_wide * BLOCK + rank) & (LANES - 1)
        for half in range(2):
            part = slice(half * LANES, (half + 1) * LANES)
            group_ref[2 * n + half : 2 * n + half + 1, :] = group[:, part]
            lane_ref[2 * n + half : 2 * n + half + 1, :] = lane[:, part]


def places(cluster_ids, owners, peers):
    whole = pl.BlockSpec(memory_space=pltpu.VMEM)
    shape = jax.ShapeDtypeStruct((cluster_ids.shape[0] // LANES, LANES), jnp.int32)
    return pl.pallas_call(
        functools.partial(place_kernel, owners, peers),
        out_shape=(shape, shape),
        in_specs=[whole],
        out_specs=(whole, whole),
        compiler_params=pltpu.CompilerParams(vmem_limit_bytes=VMEM_LIMIT),
        name="places",
    )(cluster_ids.reshape(-1, LANES))


def score_kernel(owners, rows_ref, out_ref, meta_ref, query_ref, best_ref):
    slots, width = rows_ref.shape
    tiles = slots // LANES
    for n in range(owners):
        end = (n + 1) * BLOCK
        start = (end - 1) // 16 * 16
        meta_ref[n : n + 1, :] = rows_ref[start : start + 16, :].astype(jnp.float32)[end - 1 - start : end - start, :]
    meta = meta_ref[...]
    key = meta[:, :LANES] * 65536.0 + meta[:, LANES : 2 * LANES] * 256.0 + meta[:, 2 * LANES : 3 * LANES]
    over = jnp.max(meta[:, 3 * LANES :])
    source = iota((owners, LANES), 0)

    def in_block(tile, length):
        place = tile * LANES + iota((owners, LANES), 1) - source * BLOCK
        return (place >= 0) & (place < length)

    flat = [
        jnp.sum(jnp.where(in_block(tile, SLOTS), key, 0.0), axis=0, keepdims=True) for tile in range(tiles)
    ]
    keys = jnp.concatenate(flat, axis=1)
    stacked = jnp.concatenate(flat + [jnp.zeros((LANES - tiles, LANES), jnp.float32)], axis=0)
    query_ref[...] = stacked.T
    for tile in range(tiles):
        best_ref[:, tile : tile + 1] = query_ref[:, tile : tile + 1]

    for tile in range(0, tiles, 2):
        queries = rows_ref[tile * LANES : (tile + 2) * LANES, :]
        scores = dot(queries, rows_ref[...], 1, 1)
        mine = jnp.concatenate([query_ref[:, tile : tile + 1], query_ref[:, tile + 1 : tile + 2]], axis=0)
        first = jnp.floor((mine - 1.0) * (1.0 / ORDER_SPAN)) * ORDER_SPAN
        allowed = (keys < mine) & (keys > first)
        best = jnp.max(jnp.where(allowed, scores, -float(width)), axis=1, keepdims=True) * (1.0 / width)
        best = jnp.maximum(best, -1.0)
        best_ref[:, tile : tile + 1] = best[:LANES]
        best_ref[:, tile + 1 : tile + 2] = best[LANES:]
    turned = best_ref[...].T
    result = jnp.zeros((owners, LANES), jnp.float32)
    for tile in range(tiles):
        result = jnp.where(in_block(tile, SLOTS), turned[tile : tile + 1, :], result)
        result = jnp.where(in_block(tile, BLOCK) & ~in_block(tile, SLOTS), over, result)
    out_ref[...] = result


def score(rows, owners):
    whole = pl.BlockSpec(memory_space=pltpu.VMEM)
    return pl.pallas_call(
        functools.partial(score_kernel, owners),
        out_shape=jax.ShapeDtypeStruct((owners, LANES), jnp.float32),
        in_specs=[whole],
        out_specs=whole,
        scratch_shapes=[
            pltpu.VMEM((owners, rows.shape[1]), jnp.float32),
            pltpu.VMEM((LANES, LANES), jnp.float32),
            pltpu.VMEM((LANES, LANES), jnp.float32),
        ],
        compiler_params=pltpu.CompilerParams(vmem_limit_bytes=VMEM_LIMIT),
        name="score",
    )(rows)


def pick_kernel(values_ref, group_ref, lane_ref, out_ref, over_ref):
    me_wide = lax.axis_index("wide")
    groups = values_ref.shape[0]
    values = values_ref[...]
    marked = iota((groups, LANES), 1) == ((me_wide * BLOCK + SLOTS) & (LANES - 1))
    over_ref[0, 0] = jnp.max(jnp.where(marked, values, 0.0)).astype(jnp.int32)
    turned = values.T
    high = turned.astype(jnp.bfloat16)
    rest = turned - high.astype(jnp.float32)
    middle = rest.astype(jnp.bfloat16)
    low = (rest - middle.astype(jnp.float32)).astype(jnp.bfloat16)
    parts = jnp.concatenate([high, middle, low], axis=0)
    for n in range(group_ref.shape[0] // 2):
        one_hot = jnp.where(iota((groups, CHUNK), 0) == chunk_of(group_ref, n), 1.0, 0.0).astype(jnp.bfloat16)
        by_lane = dot(parts, one_hot, 1, 0)
        by_lane = by_lane[:LANES] + by_lane[LANES : 2 * LANES] + by_lane[2 * LANES :]
        here = iota((LANES, CHUNK), 0) == chunk_of(lane_ref, n)
        picked = jnp.sum(jnp.where(here, by_lane, 0.0), axis=0, keepdims=True)
        out_ref[2 * n : 2 * n + 1, :] = picked[:, :LANES]
        out_ref[2 * n + 1 : 2 * n + 2, :] = picked[:, LANES:]


def pick(values, group, lane):
    whole = pl.BlockSpec(memory_space=pltpu.VMEM)
    return pl.pallas_call(
        pick_kernel,
        out_shape=(
            jax.ShapeDtypeStruct(group.shape, jnp.float32),
            jax.ShapeDtypeStruct((1, 1), jnp.int32),
        ),
        in_specs=[whole, whole, whole],
        out_specs=(whole, pl.BlockSpec(memory_space=pltpu.SMEM)),
        compiler_params=pltpu.CompilerParams(vmem_limit_bytes=VMEM_LIMIT),
        name="pick",
    )(values, group, lane)


def unit_vectors(row_codes, row_scales, row_biases):
    values = row_codes.astype(jnp.float32) * row_scales[:, None] + row_biases[:, None]
    return (values * lax.rsqrt(jnp.mean(values * values, axis=1, keepdims=True) + epsilon)).astype(
        jnp.bfloat16
    )


def fold_block(
    queries, query_cluster, query_order, running, block_rows, block_cluster, block_order
):
    feature_width = queries.shape[-1]
    scores = (
        jnp.einsum("qe,ke->qk", queries, block_rows, preferred_element_type=jnp.float32)
        / feature_width
    )
    allowed = (query_cluster[:, None] == block_cluster[None, :]) & (
        block_order[None, :] < query_order[:, None]
    )
    return jnp.maximum(running, jnp.max(jnp.where(allowed, scores, -1.0), axis=1))


def fold_keys(
    queries, query_cluster, query_order, share_rows, running, piece_rows, piece_cluster, piece_order
):
    feature_width = piece_rows.shape[2]
    blocks = piece_rows.shape[1] // share_rows

    def visit_block(block_index, best_now):
        start_col = block_index * share_rows
        block_rows = lax.dynamic_slice_in_dim(piece_rows, start_col, share_rows, 1).reshape(
            -1, feature_width
        )
        block_cluster = lax.dynamic_slice_in_dim(piece_cluster, start_col, share_rows, 1).reshape(
            -1
        )
        block_order = lax.dynamic_slice_in_dim(piece_order, start_col, share_rows, 1).reshape(-1)
        return fold_block(
            queries, query_cluster, query_order, best_now, block_rows, block_cluster, block_order
        )

    return lax.fori_loop(0, blocks, visit_block, running)


def any_skew(row_codes, row_scales, row_biases, cluster_ids, order_index):
    owners = lax.axis_size("wide")
    peer_count = lax.axis_size("narrow")
    local_rows = row_codes.shape[0]
    feature_width = row_codes.shape[1]
    capacity = 2 * local_rows // owners
    share_rows = capacity // peer_count
    total_slots = owners * capacity
    unit_rows = unit_vectors(row_codes, row_scales, row_biases)
    owner_of = cluster_ids % owners
    one_hot = (owner_of[:, None] == jnp.arange(owners, dtype=jnp.int32)[None, :]).astype(jnp.int32)
    before = jnp.cumsum(one_hot, axis=0) - one_hot
    slot_rank = jnp.sum(before * one_hot, axis=1)
    slot_index = owner_of * capacity + slot_rank
    send_rows = jnp.zeros((total_slots, feature_width), jnp.bfloat16).at[slot_index].set(unit_rows)
    send_rows = send_rows.reshape(owners, capacity, feature_width)
    send_cluster = (
        jnp.full((total_slots,), -1, jnp.int32)
        .at[slot_index]
        .set(cluster_ids)
        .reshape(owners, capacity)
    )
    send_order = (
        jnp.full((total_slots,), -1, jnp.int32)
        .at[slot_index]
        .set(order_index)
        .reshape(owners, capacity)
    )
    offset = lax.axis_index("narrow") * share_rows
    initial = jnp.full((owners * share_rows,), -1.0, jnp.float32)
    got_rows, got_cluster, got_order = (
        lax.all_to_all(send_rows, "wide", split_axis=0, concat_axis=0, tiled=True),
        lax.all_to_all(send_cluster, "wide", split_axis=0, concat_axis=0, tiled=True),
        lax.all_to_all(send_order, "wide", split_axis=0, concat_axis=0, tiled=True),
    )
    queries = lax.dynamic_slice_in_dim(got_rows, offset, share_rows, 1).reshape(-1, feature_width)
    query_cluster = lax.dynamic_slice_in_dim(got_cluster, offset, share_rows, 1).reshape(-1)
    query_order = lax.dynamic_slice_in_dim(got_order, offset, share_rows, 1).reshape(-1)
    best_sim = fold_keys(
        queries, query_cluster, query_order, share_rows, initial, got_rows, got_cluster, got_order
    )
    column = lax.all_gather(best_sim.reshape(owners, share_rows), "narrow", axis=1, tiled=True)
    returned = lax.all_to_all(column, "wide", split_axis=0, concat_axis=0, tiled=True)
    return returned.reshape(-1)[slot_index]


def shards(row_codes, row_scales, row_biases, cluster_ids, order_index):
    owners = lax.axis_size("wide")
    peers = lax.axis_size("narrow")
    width = row_codes.shape[1]
    sent = pack(row_codes, row_scales, row_biases, cluster_ids, order_index, owners, peers)
    got = lax.all_to_all(
        sent.reshape(owners, BLOCK, width), "wide", split_axis=0, concat_axis=0, tiled=True
    ).reshape(owners * BLOCK, width)
    group, lane = places(cluster_ids, owners, peers)
    best = score(got, owners)
    back = lax.all_to_all(best.reshape(owners, 1, LANES), "wide", split_axis=0, concat_axis=0, tiled=True)
    values = lax.all_gather(back.reshape(owners, LANES), "narrow", axis=0, tiled=True)
    picked, over = pick(values, group, lane)
    return lax.cond(
        over[0, 0] > 0,
        lambda: any_skew(row_codes, row_scales, row_biases, cluster_ids, order_index),
        lambda: picked.reshape(-1),
    )


def solution(mesh):
    in_specs = (P("wide", None), P("wide"), P("wide"), P("wide"), P("wide"))
    out_specs = P("wide")
    return jax.shard_map(shards, mesh=mesh, in_specs=in_specs, out_specs=out_specs, check_vma=False)
```

```python
import functools

import jax
import jax.numpy as jnp
from jax import lax
from jax.experimental import pallas as pl
from jax.experimental.pallas import tpu as pltpu
from jax.sharding import PartitionSpec as P

epsilon = 1e-06

BLOCK = 48
SLOTS = BLOCK - 1
LANES = 128
HALF = LANES // 2
CHUNK = 256
ORDER_SPAN = 131072
VMEM_LIMIT = 48 * 1024 * 1024


def iota(shape, axis):
    return lax.broadcasted_iota(jnp.int32, shape, axis)


def dot(left, right, left_axis, right_axis):
    return lax.dot_general(
        left, right, (((left_axis,), (right_axis,)), ((), ())), preferred_element_type=jnp.float32
    )


def strictly_before():
    return (iota((CHUNK, CHUNK), 0) < iota((CHUNK, CHUNK), 1)).astype(jnp.bfloat16)


def chunk_of(ref, index):
    return jnp.concatenate([ref[2 * index : 2 * index + 1, :], ref[2 * index + 1 : 2 * index + 2, :]], axis=1)


def owner_and_chip(clusters, owners, peers):
    owner = clusters & (owners - 1)
    place = clusters >> (owners.bit_length() - 1)
    chip = jnp.minimum(place, 2 * peers - 1 - place) >> 1
    return owner, place, chip


def pack_kernel(
    owners, peers, cluster_ref, order_ref, scale_ref, bias_ref, codes_hbm, out_ref,
    codes_half, codes_full, slots_full, table_vmem, table_smem, code_sems, table_sem,
):
    local_rows = codes_hbm.shape[0]
    me_wide = lax.axis_index("wide")
    me_narrow = lax.axis_index("narrow")
    pieces = code_sems.shape[0]
    piece = local_rows // pieces
    copies = [
        pltpu.make_async_copy(
            codes_hbm.at[pl.ds(n * piece, piece)], codes_half.at[pl.ds(n * piece, piece)], code_sems.at[n]
        )
        for n in range(pieces)
    ]
    for copy in copies:
        copy.start()

    before = strictly_before()
    count = jnp.zeros((owners, 1), jnp.float32)
    table = jnp.zeros((owners, 3 * LANES), jnp.float32)
    for n in range(local_rows // CHUNK):
        clusters = chunk_of(cluster_ref, n)
        orders = chunk_of(order_ref, n)
        owner, place, chip = owner_and_chip(clusters, owners, peers)
        owner = jnp.where(chip == me_narrow >> 1, owner, -1)
        mine = iota((owners, CHUNK), 0) == owner
        one_hot = jnp.where(mine, 1.0, 0.0)
        one_hot_half = one_hot.astype(jnp.bfloat16)
        earlier = dot(one_hot_half, before, 1, 0) + count
        rank = jnp.sum(jnp.where(mine, earlier, 0.0), axis=0, keepdims=True).astype(jnp.int32)
        count = count + jnp.sum(one_hot, axis=1, keepdims=True)
        slot = jnp.where((rank & 1) == (me_narrow & 1), rank >> 1, -1)
        key = place * ORDER_SPAN + orders + 1
        row = n * CHUNK + iota((1, CHUNK), 1)
        at_slot = iota((HALF, CHUNK), 0) == slot
        parts = [
            jnp.where(at_slot, part.astype(jnp.float32), 0.0).astype(jnp.bfloat16)
            for part in (row >> 6, row & 63, key >> 16, (key >> 8) & 255, key & 255)
        ]
        parts.append(jnp.zeros((HALF, CHUNK), jnp.bfloat16))
        table = table + dot(one_hot_half, jnp.concatenate(parts, axis=0), 1, 1)
    lane = iota((owners, LANES), 1)
    rows_at = table[:, :LANES] * 64.0 + pltpu.roll(table[:, :LANES], HALF, 1)
    used = jnp.minimum((count.astype(jnp.int32) + 1 - (me_narrow & 1)) >> 1, SLOTS)
    table_vmem[...] = jnp.where(lane == HALF, used, rows_at.astype(jnp.int32))
    table_copy = pltpu.make_async_copy(table_vmem, table_smem, table_sem)
    table_copy.start()
    turn = me_wide * BLOCK
    first = jnp.where(lane < HALF, table[:, LANES : 2 * LANES], 0.0)
    second = jnp.where(lane < HALF, 0.0, table[:, LANES : 2 * LANES])
    third = table[:, 2 * LANES :]
    over = jnp.where(jnp.max(count) > 2 * SLOTS, 1.0, 0.0)
    meta = jnp.concatenate(
        [
            pltpu.roll(first, turn & (LANES - 1), 1),
            pltpu.roll(second, (turn + HALF) & (LANES - 1), 1),
            pltpu.roll(third, turn & (LANES - 1), 1),
            jnp.full((owners, LANES), over, jnp.float32),
        ],
        axis=1,
    )

    slots_full[...] = jnp.zeros_like(slots_full)
    for n, copy in enumerate(copies):
        copy.wait()
        codes_full[n * piece : (n + 1) * piece, :] = codes_half[n * piece : (n + 1) * piece, :].astype(jnp.float32)
    table_copy.wait()

    def two_owners(half, carry):
        pair = (2 * half, 2 * half + 1)
        used = jnp.maximum(table_smem[pair[0], HALF], table_smem[pair[1], HALF])

        def eight_rows(group, carry):
            for owner in pair:
                for n in range(8):
                    slot = group * 8 + n
                    row = table_smem[owner, slot]
                    slots_full[pl.ds(owner * BLOCK + slot, 1), :] = (
                        codes_full[pl.ds(row, 1), :] * scale_ref[row] + bias_ref[row]
                    )
            return carry

        return lax.fori_loop(0, (used + 7) // 8, eight_rows, carry)

    lax.fori_loop(0, owners // 2, two_owners, 0)

    pair = 2 * BLOCK
    for n in range(owners // 2):
        values = slots_full[n * pair : (n + 1) * pair, :]
        mean_square = jnp.mean(values * values, axis=1, keepdims=True)
        unit = values * lax.rsqrt(mean_square + epsilon)
        place = iota((pair, 1), 0)
        unit = jnp.where(place == SLOTS, meta[2 * n : 2 * n + 1], unit)
        unit = jnp.where(place == BLOCK + SLOTS, meta[2 * n + 1 : 2 * n + 2], unit)
        out_ref[n * pair : (n + 1) * pair, :] = unit.astype(jnp.bfloat16)


def pack(row_codes, row_scales, row_biases, cluster_ids, order_index, owners, peers):
    local_rows, width = row_codes.shape
    whole = pl.BlockSpec(memory_space=pltpu.VMEM)
    scalars = pl.BlockSpec(memory_space=pltpu.SMEM)
    pieces = 8
    return pl.pallas_call(
        functools.partial(pack_kernel, owners, peers),
        out_shape=jax.ShapeDtypeStruct((owners * BLOCK, width), jnp.bfloat16),
        in_specs=[whole, whole, scalars, scalars, pl.BlockSpec(memory_space=pl.ANY)],
        out_specs=whole,
        scratch_shapes=[
            pltpu.VMEM((local_rows, width), jnp.bfloat16),
            pltpu.VMEM((local_rows, width), jnp.float32),
            pltpu.VMEM((owners * BLOCK, width), jnp.float32),
            pltpu.VMEM((owners, LANES), jnp.int32),
            pltpu.SMEM((owners, LANES), jnp.int32),
            pltpu.SemaphoreType.DMA((pieces,)),
            pltpu.SemaphoreType.DMA,
        ],
        compiler_params=pltpu.CompilerParams(vmem_limit_bytes=VMEM_LIMIT),
        name="pack",
    )(
        cluster_ids.reshape(-1, LANES), order_index.reshape(-1, LANES), row_scales, row_biases, row_codes,
    )


def place_kernel(owners, peers, cluster_ref, group_ref, lane_ref):
    me_wide = lax.axis_index("wide")
    groups = owners * peers // 2
    before = strictly_before()
    count = jnp.zeros((groups, 1), jnp.float32)
    for n in range(cluster_ref.shape[0] // 2):
        owner, _, chip = owner_and_chip(chunk_of(cluster_ref, n), owners, peers)
        mine = iota((groups, CHUNK), 0) == chip * owners + owner
        one_hot = jnp.where(mine, 1.0, 0.0)
        earlier = dot(one_hot.astype(jnp.bfloat16), before, 1, 0) + count
        rank = jnp.sum(jnp.where(mine, earlier, 0.0), axis=0, keepdims=True).astype(jnp.int32)
        count = count + jnp.sum(one_hot, axis=1, keepdims=True)
        group = (2 * chip + (rank & 1)) * owners + owner
        lane = (me_wide * BLOCK + (rank >> 1)) & (LANES - 1)
        for half in range(2):
            part = slice(half * LANES, (half + 1) * LANES)
            group_ref[2 * n + half : 2 * n + half + 1, :] = group[:, part]
            lane_ref[2 * n + half : 2 * n + half + 1, :] = lane[:, part]


def places(cluster_ids, owners, peers):
    whole = pl.BlockSpec(memory_space=pltpu.VMEM)
    shape = jax.ShapeDtypeStruct((cluster_ids.shape[0] // LANES, LANES), jnp.int32)
    return pl.pallas_call(
        functools.partial(place_kernel, owners, peers),
        out_shape=(shape, shape),
        in_specs=[whole],
        out_specs=(whole, whole),
        compiler_params=pltpu.CompilerParams(vmem_limit_bytes=VMEM_LIMIT),
        name="places",
    )(cluster_ids.reshape(-1, LANES))


def in_block(owners, tile, length):
    place = tile * LANES + iota((owners, LANES), 1) - iota((owners, LANES), 0) * BLOCK
    return (place >= 0) & (place < length)


def keys_of(owners, rows_ref, meta_ref):
    for n in range(owners):
        end = (n + 1) * BLOCK
        meta_ref[n : n + 1, :] = rows_ref[end - 16 : end, :].astype(jnp.float32)[15:16, :]
    meta = meta_ref[...]
    key = meta[:, :LANES] * 65536.0 + meta[:, LANES : 2 * LANES] * 256.0 + meta[:, 2 * LANES : 3 * LANES]
    flat = [
        jnp.sum(jnp.where(in_block(owners, tile, SLOTS), key, 0.0), axis=0, keepdims=True)
        for tile in range(rows_ref.shape[0] // LANES)
    ]
    return flat, jnp.max(meta[:, 3 * LANES :])


def fold(rows_ref, key_rows_ref, keys, query_ref, best_in, best_ref):
    slots, width = rows_ref.shape
    for tile in range(0, slots // LANES, 2):
        scores = dot(rows_ref[tile * LANES : (tile + 2) * LANES, :], key_rows_ref[...], 1, 1)
        mine = jnp.concatenate([query_ref[:, tile : tile + 1], query_ref[:, tile + 1 : tile + 2]], axis=0)
        first = jnp.floor((mine - 1.0) * (1.0 / ORDER_SPAN)) * ORDER_SPAN
        allowed = (keys < mine) & (keys > first)
        best = jnp.max(jnp.where(allowed, scores, -float(width)), axis=1, keepdims=True) * (1.0 / width)
        best = jnp.maximum(best, -1.0)
        for half in range(2):
            part = best[half * LANES : (half + 1) * LANES]
            if best_in is not None:
                part = jnp.maximum(part, best_in[:, tile + half : tile + half + 1])
            best_ref[:, tile + half : tile + half + 1] = part


def own_kernel(owners, rows_ref, query_ref, best_ref, meta_ref):
    flat, _ = keys_of(owners, rows_ref, meta_ref)
    query_ref[...] = jnp.concatenate(
        flat + [jnp.zeros((LANES - len(flat), LANES), jnp.float32)], axis=0
    ).T
    fold(rows_ref, rows_ref, jnp.concatenate(flat, axis=1), query_ref, None, best_ref)


def other_kernel(owners, rows_ref, other_ref, query_ref, best_in, out_ref, meta_ref, best_ref):
    flat, over = keys_of(owners, other_ref, meta_ref)
    fold(rows_ref, other_ref, jnp.concatenate(flat, axis=1), query_ref, best_in, best_ref)
    turned = best_ref[...].T
    result = jnp.zeros((owners, LANES), jnp.float32)
    for tile in range(len(flat)):
        result = jnp.where(in_block(owners, tile, SLOTS), turned[tile : tile + 1, :], result)
        result = jnp.where(in_block(owners, tile, BLOCK) & ~in_block(owners, tile, SLOTS), over, result)
    out_ref[...] = result


def score(rows, owners):
    slots, width = rows.shape
    whole = pl.BlockSpec(memory_space=pltpu.VMEM)
    square = jax.ShapeDtypeStruct((LANES, LANES), jnp.float32)
    cost = pl.CostEstimate(
        flops=2 * slots * slots * width, bytes_accessed=4 * slots * width, transcendentals=0
    )
    peers = lax.axis_size("narrow")
    other = lax.ppermute(rows, "narrow", [(n, n ^ 1) for n in range(peers)])
    meta = pltpu.VMEM((owners, width), jnp.float32)
    params = pltpu.CompilerParams(vmem_limit_bytes=VMEM_LIMIT)
    query, best = pl.pallas_call(
        functools.partial(own_kernel, owners),
        out_shape=(square, square),
        in_specs=[whole],
        out_specs=(whole, whole),
        scratch_shapes=[meta],
        compiler_params=params,
        cost_estimate=cost,
        name="score_own",
    )(rows)
    return pl.pallas_call(
        functools.partial(other_kernel, owners),
        out_shape=jax.ShapeDtypeStruct((owners, LANES), jnp.float32),
        in_specs=[whole] * 4,
        out_specs=whole,
        scratch_shapes=[meta, pltpu.VMEM((LANES, LANES), jnp.float32)],
        compiler_params=params,
        cost_estimate=cost,
        name="score_other",
    )(rows, other, query, best)


def pick_kernel(values_ref, group_ref, lane_ref, out_ref, over_ref):
    me_wide = lax.axis_index("wide")
    groups = values_ref.shape[0]
    values = values_ref[...]
    marked = iota((groups, LANES), 1) == ((me_wide * BLOCK + SLOTS) & (LANES - 1))
    over_ref[0, 0] = jnp.max(jnp.where(marked, values, 0.0)).astype(jnp.int32)
    turned = values.T
    high = turned.astype(jnp.bfloat16)
    rest = turned - high.astype(jnp.float32)
    middle = rest.astype(jnp.bfloat16)
    low = (rest - middle.astype(jnp.float32)).astype(jnp.bfloat16)
    parts = jnp.concatenate([high, middle, low], axis=0)
    for n in range(group_ref.shape[0] // 2):
        one_hot = jnp.where(iota((groups, CHUNK), 0) == chunk_of(group_ref, n), 1.0, 0.0).astype(jnp.bfloat16)
        by_lane = dot(parts, one_hot, 1, 0)
        by_lane = by_lane[:LANES] + by_lane[LANES : 2 * LANES] + by_lane[2 * LANES :]
        here = iota((LANES, CHUNK), 0) == chunk_of(lane_ref, n)
        picked = jnp.sum(jnp.where(here, by_lane, 0.0), axis=0, keepdims=True)
        out_ref[2 * n : 2 * n + 1, :] = picked[:, :LANES]
        out_ref[2 * n + 1 : 2 * n + 2, :] = picked[:, LANES:]


def pick(values, group, lane):
    whole = pl.BlockSpec(memory_space=pltpu.VMEM)
    return pl.pallas_call(
        pick_kernel,
        out_shape=(
            jax.ShapeDtypeStruct(group.shape, jnp.float32),
            jax.ShapeDtypeStruct((1, 1), jnp.int32),
        ),
        in_specs=[whole, whole, whole],
        out_specs=(whole, pl.BlockSpec(memory_space=pltpu.SMEM)),
        compiler_params=pltpu.CompilerParams(vmem_limit_bytes=VMEM_LIMIT),
        name="pick",
    )(values, group, lane)


def unit_vectors(row_codes, row_scales, row_biases):
    values = row_codes.astype(jnp.float32) * row_scales[:, None] + row_biases[:, None]
    return (values * lax.rsqrt(jnp.mean(values * values, axis=1, keepdims=True) + epsilon)).astype(
        jnp.bfloat16
    )


def fold_block(
    queries, query_cluster, query_order, running, block_rows, block_cluster, block_order
):
    feature_width = queries.shape[-1]
    scores = (
        jnp.einsum("qe,ke->qk", queries, block_rows, preferred_element_type=jnp.float32)
        / feature_width
    )
    allowed = (query_cluster[:, None] == block_cluster[None, :]) & (
        block_order[None, :] < query_order[:, None]
    )
    return jnp.maximum(running, jnp.max(jnp.where(allowed, scores, -1.0), axis=1))


def fold_keys(
    queries, query_cluster, query_order, share_rows, running, piece_rows, piece_cluster, piece_order
):
    feature_width = piece_rows.shape[2]
    blocks = piece_rows.shape[1] // share_rows

    def visit_block(block_index, best_now):
        start_col = block_index * share_rows
        block_rows = lax.dynamic_slice_in_dim(piece_rows, start_col, share_rows, 1).reshape(
            -1, feature_width
        )
        block_cluster = lax.dynamic_slice_in_dim(piece_cluster, start_col, share_rows, 1).reshape(
            -1
        )
        block_order = lax.dynamic_slice_in_dim(piece_order, start_col, share_rows, 1).reshape(-1)
        return fold_block(
            queries, query_cluster, query_order, best_now, block_rows, block_cluster, block_order
        )

    return lax.fori_loop(0, blocks, visit_block, running)


def any_skew(row_codes, row_scales, row_biases, cluster_ids, order_index):
    owners = lax.axis_size("wide")
    peer_count = lax.axis_size("narrow")
    local_rows = row_codes.shape[0]
    feature_width = row_codes.shape[1]
    capacity = 2 * local_rows // owners
    share_rows = capacity // peer_count
    total_slots = owners * capacity
    unit_rows = unit_vectors(row_codes, row_scales, row_biases)
    owner_of = cluster_ids % owners
    one_hot = (owner_of[:, None] == jnp.arange(owners, dtype=jnp.int32)[None, :]).astype(jnp.int32)
    before = jnp.cumsum(one_hot, axis=0) - one_hot
    slot_rank = jnp.sum(before * one_hot, axis=1)
    slot_index = owner_of * capacity + slot_rank
    send_rows = jnp.zeros((total_slots, feature_width), jnp.bfloat16).at[slot_index].set(unit_rows)
    send_rows = send_rows.reshape(owners, capacity, feature_width)
    send_cluster = (
        jnp.full((total_slots,), -1, jnp.int32)
        .at[slot_index]
        .set(cluster_ids)
        .reshape(owners, capacity)
    )
    send_order = (
        jnp.full((total_slots,), -1, jnp.int32)
        .at[slot_index]
        .set(order_index)
        .reshape(owners, capacity)
    )
    offset = lax.axis_index("narrow") * share_rows
    initial = jnp.full((owners * share_rows,), -1.0, jnp.float32)
    got_rows, got_cluster, got_order = (
        lax.all_to_all(send_rows, "wide", split_axis=0, concat_axis=0, tiled=True),
        lax.all_to_all(send_cluster, "wide", split_axis=0, concat_axis=0, tiled=True),
        lax.all_to_all(send_order, "wide", split_axis=0, concat_axis=0, tiled=True),
    )
    queries = lax.dynamic_slice_in_dim(got_rows, offset, share_rows, 1).reshape(-1, feature_width)
    query_cluster = lax.dynamic_slice_in_dim(got_cluster, offset, share_rows, 1).reshape(-1)
    query_order = lax.dynamic_slice_in_dim(got_order, offset, share_rows, 1).reshape(-1)
    best_sim = fold_keys(
        queries, query_cluster, query_order, share_rows, initial, got_rows, got_cluster, got_order
    )
    column = lax.all_gather(best_sim.reshape(owners, share_rows), "narrow", axis=1, tiled=True)
    returned = lax.all_to_all(column, "wide", split_axis=0, concat_axis=0, tiled=True)
    return returned.reshape(-1)[slot_index]


def shards(row_codes, row_scales, row_biases, cluster_ids, order_index):
    owners = lax.axis_size("wide")
    peers = lax.axis_size("narrow")
    width = row_codes.shape[1]
    sent = pack(row_codes, row_scales, row_biases, cluster_ids, order_index, owners, peers)
    got = lax.all_to_all(
        sent.reshape(owners, BLOCK, width), "wide", split_axis=0, concat_axis=0, tiled=True
    ).reshape(owners * BLOCK, width)
    group, lane = places(cluster_ids, owners, peers)
    best = score(got, owners)
    back = lax.all_to_all(best.reshape(owners, 1, LANES), "wide", split_axis=0, concat_axis=0, tiled=True)
    copies = jnp.broadcast_to(back.reshape(1, owners, LANES), (peers, owners, LANES))
    values = lax.all_to_all(copies, "narrow", split_axis=0, concat_axis=0, tiled=True)
    values = values.reshape(peers * owners, LANES)
    picked, over = pick(values, group, lane)
    _, result = lax.while_loop(
        lambda state: state[0] > 0,
        lambda state: (
            jnp.zeros_like(state[0]),
            any_skew(row_codes, row_scales, row_biases, cluster_ids, order_index),
        ),
        (over[0, 0], picked.reshape(-1)),
    )
    return result


def solution(mesh):
    in_specs = (P("wide", None), P("wide"), P("wide"), P("wide"), P("wide"))
    out_specs = P("wide")
    return jax.shard_map(shards, mesh=mesh, in_specs=in_specs, out_specs=out_specs, check_vma=False)
```

```python
import functools

import jax
import jax.numpy as jnp
from jax import lax
from jax.experimental import pallas as pl
from jax.experimental.pallas import tpu as pltpu
from jax.sharding import PartitionSpec as P

epsilon = 1e-06

BLOCK = 40
SLOTS = BLOCK - 1
LANES = 128
HALF = LANES // 2
PITCH = 5
TABLE = 48
TAKE = 4
CHUNK = 256
ORDER_SPAN = 131072
VMEM_LIMIT = 48 * 1024 * 1024


def iota(shape, axis):
    return lax.broadcasted_iota(jnp.int32, shape, axis)


def dot(left, right, left_axis, right_axis):
    return lax.dot_general(
        left, right, (((left_axis,), (right_axis,)), ((), ())), preferred_element_type=jnp.float32
    )


def strictly_before():
    return (iota((CHUNK, CHUNK), 0) < iota((CHUNK, CHUNK), 1)).astype(jnp.bfloat16)


def chunk_of(ref, index):
    return jnp.concatenate([ref[2 * index : 2 * index + 1, :], ref[2 * index + 1 : 2 * index + 2, :]], axis=1)


def split(clusters, owners):
    return clusters & (owners - 1), clusters >> (owners.bit_length() - 1)


def busiest_owner(cluster_ref, owners):
    total = jnp.zeros((owners, CHUNK), jnp.float32)
    for n in range(cluster_ref.shape[0] // 2):
        owner, _ = split(chunk_of(cluster_ref, n), owners)
        total = total + jnp.where(iota((owners, CHUNK), 0) == owner, 1.0, 0.0)
    total = jnp.sum(total, axis=1, keepdims=True)
    at_top = total == jnp.max(total, axis=0, keepdims=True)
    return jnp.min(jnp.where(at_top, iota((owners, 1), 0), owners), axis=0, keepdims=True)


def owner_place_chip(clusters, owners, peers, busiest):
    owner, place = split(clusters, owners)
    chip = jnp.minimum(place, 2 * peers - 1 - place) >> 1
    busy = owner == busiest
    lent = busy & (place >= 4) & (place < 8)
    busy_chip = jnp.where(place >= 12, 3 - (place & 3), place & 3)
    chip = jnp.where(lent, (place - 4) >> 1, jnp.where(busy, busy_chip, chip))
    owner = jnp.where(lent, (owner + place - 3) & (owners - 1), owner)
    return owner, place, chip


def pack_kernel(
    owners, peers, cluster_ref, order_ref, scale_hbm, bias_hbm, codes_hbm, out_ref,
    codes_half, codes_full, slots_full, table_vmem, table_smem, scale_ref, bias_ref, code_sems, small_sems,
):
    local_rows = codes_hbm.shape[0]
    me_wide = lax.axis_index("wide")
    me_narrow = lax.axis_index("narrow")
    pieces = code_sems.shape[0]
    tiles = codes_hbm.shape[1] // LANES
    piece = local_rows // pieces
    copies = [
        pltpu.make_async_copy(
            codes_hbm.at[pl.ds(n * piece, piece)], codes_half.at[pl.ds(n * piece, piece)], code_sems.at[n]
        )
        for n in range(pieces)
    ]
    small_copies = [
        pltpu.make_async_copy(scale_hbm, scale_ref, small_sems.at[0]),
        pltpu.make_async_copy(bias_hbm, bias_ref, small_sems.at[1]),
    ]
    for copy in copies + small_copies:
        copy.start()

    chunks = local_rows // CHUNK
    busiest = busiest_owner(cluster_ref, owners)
    places, masks, hots = [], [], []
    for n in range(chunks):
        owner, place, chip = owner_place_chip(chunk_of(cluster_ref, n), owners, peers, busiest)
        mask = iota((owners, CHUNK), 0) == jnp.where(chip == me_narrow >> 1, owner, -1)
        places.append(place)
        masks.append(mask)
        hots.append(jnp.where(mask, 1.0, 0.0))
    earlier = dot(jnp.concatenate(hots, axis=0).astype(jnp.bfloat16), strictly_before(), 1, 0)
    count = jnp.zeros((owners, 1), jnp.float32)
    spread = []
    for n in range(chunks):
        within = earlier[n * owners : (n + 1) * owners]
        rank = jnp.sum(jnp.where(masks[n], within + count, 0.0), axis=0, keepdims=True).astype(jnp.int32)
        count = count + within[:, CHUNK - 1 :] + hots[n][:, CHUNK - 1 :]
        slot = jnp.where((rank & 1) == (me_narrow & 1), rank >> 1, -1)
        key = places[n] * ORDER_SPAN + chunk_of(order_ref, n) + 1
        row = n * CHUNK + iota((1, CHUNK), 1)
        at_slot = iota((TABLE, CHUNK), 0) == slot
        parts = [
            jnp.where(at_slot, part.astype(jnp.float32), 0.0).astype(jnp.bfloat16)
            for part in (row >> 6, row & 63, key >> 16, (key >> 8) & 255, key & 255)
        ]
        spread.append(jnp.concatenate(parts, axis=0))
    table = dot(
        jnp.concatenate(spread, axis=1), jnp.concatenate(hots, axis=1).astype(jnp.bfloat16), 1, 1
    )
    rows_at = table[:TABLE] * 64.0 + table[TABLE : 2 * TABLE]
    wide = jnp.concatenate([count, jnp.zeros((owners, LANES - 1), jnp.float32)], axis=1)
    counts = jnp.concatenate([wide, jnp.zeros((LANES - owners, LANES), jnp.float32)], axis=0).T[:1, :owners]
    used = jnp.minimum((counts.astype(jnp.int32) + 1 - (me_narrow & 1)) >> 1, SLOTS)
    table_vmem[:, :owners] = jnp.concatenate(
        [rows_at.astype(jnp.int32), jnp.broadcast_to(used, (8, owners))], axis=0
    )
    table_copy = pltpu.make_async_copy(table_vmem, table_smem, small_sems.at[2])
    table_copy.start()
    over = jnp.where(jnp.max(count) > 2 * SLOTS, 1.0, 0.0)
    turn = (me_wide * BLOCK) & (LANES - 1)
    meta = []
    for n in range(2, 5):
        part = jnp.concatenate(
            [table[n * TABLE : n * TABLE + SLOTS + 1], jnp.zeros((LANES - BLOCK, owners), jnp.float32)], axis=0
        )
        part = jnp.concatenate([part, jnp.zeros((LANES, LANES - owners), jnp.float32)], axis=1).T
        meta.append(pltpu.roll(part[:owners], turn, 1))
    lane = iota((owners, LANES), 1)
    meta.append(jnp.where(lane < HALF, over, busiest.astype(jnp.float32)))

    slots_full[...] = jnp.zeros_like(slots_full)
    for n, copy in enumerate(copies):
        copy.wait()
        values = codes_half[n * piece : (n + 1) * piece, :].astype(jnp.float32)
        for tile in range(tiles):
            codes_full[pl.ds(n * piece * PITCH + tile, piece, stride=PITCH), :] = values[
                :, tile * LANES : (tile + 1) * LANES
            ]
    for copy in [table_copy] + small_copies:
        copy.wait()

    def two_owners(half, carry):
        pair = (2 * half, 2 * half + 1)
        used = jnp.maximum(table_smem[TABLE, pair[0]], table_smem[TABLE, pair[1]])

        def eight_rows(group, carry):
            for owner in pair:
                for n in range(8):
                    slot = group * 8 + n
                    row = table_smem[slot, owner]
                    slots_full[pl.ds((owner * BLOCK + slot) * PITCH, TAKE), :] = (
                        codes_full[pl.ds(row * PITCH, TAKE), :] * scale_ref[row]
                        + bias_ref[row]
                    )
            return carry

        return lax.fori_loop(0, (used + 7) // 8, eight_rows, carry)

    lax.fori_loop(0, owners // 2, two_owners, 0)

    pair = 2 * BLOCK
    width = tiles * LANES
    for n in range(owners // 2):
        values = [
            slots_full[pl.ds(n * pair * PITCH + tile, pair, stride=PITCH), :] for tile in range(tiles)
        ]
        squares = functools.reduce(jnp.add, [value * value for value in values])
        mean_square = jnp.sum(squares, axis=1, keepdims=True) * (1.0 / width)
        factor = lax.rsqrt(mean_square + epsilon)
        place = iota((pair, 1), 0)
        for tile in range(tiles):
            unit = values[tile] * factor
            unit = jnp.where(place == SLOTS, meta[tile][2 * n : 2 * n + 1], unit)
            unit = jnp.where(place == BLOCK + SLOTS, meta[tile][2 * n + 1 : 2 * n + 2], unit)
            out_ref[n * pair : (n + 1) * pair, tile * LANES : (tile + 1) * LANES] = unit.astype(jnp.bfloat16)


def pack(row_codes, row_scales, row_biases, cluster_ids, order_index, owners, peers):
    local_rows, width = row_codes.shape
    whole = pl.BlockSpec(memory_space=pltpu.VMEM)
    outside = pl.BlockSpec(memory_space=pl.ANY)
    pieces = 8
    return pl.pallas_call(
        functools.partial(pack_kernel, owners, peers),
        out_shape=jax.ShapeDtypeStruct((owners * BLOCK, width), jnp.bfloat16),
        in_specs=[whole, whole, outside, outside, outside],
        out_specs=whole,
        scratch_shapes=[
            pltpu.VMEM((local_rows, width), jnp.bfloat16),
            pltpu.VMEM((local_rows * PITCH, LANES), jnp.float32),
            pltpu.VMEM((owners * BLOCK * PITCH, LANES), jnp.float32),
            pltpu.VMEM((TABLE + 8, LANES), jnp.int32),
            pltpu.SMEM((TABLE + 8, LANES), jnp.int32),
            pltpu.SMEM((local_rows,), jnp.float32),
            pltpu.SMEM((local_rows,), jnp.float32),
            pltpu.SemaphoreType.DMA((pieces,)),
            pltpu.SemaphoreType.DMA((3,)),
        ],
        compiler_params=pltpu.CompilerParams(vmem_limit_bytes=VMEM_LIMIT),
        name="pack",
    )(
        cluster_ids.reshape(-1, LANES), order_index.reshape(-1, LANES), row_scales, row_biases, row_codes,
    )


def place_kernel(owners, peers, cluster_ref, group_ref, lane_ref):
    me_wide = lax.axis_index("wide")
    groups = owners * peers // 2
    before = strictly_before()
    count = jnp.zeros((groups, 1), jnp.float32)
    busiest = busiest_owner(cluster_ref, owners)
    for n in range(cluster_ref.shape[0] // 2):
        owner, _, chip = owner_place_chip(chunk_of(cluster_ref, n), owners, peers, busiest)
        mine = iota((groups, CHUNK), 0) == chip * owners + owner
        one_hot = jnp.where(mine, 1.0, 0.0)
        earlier = dot(one_hot.astype(jnp.bfloat16), before, 1, 0) + count
        rank = jnp.sum(jnp.where(mine, earlier, 0.0), axis=0, keepdims=True).astype(jnp.int32)
        count = count + jnp.sum(one_hot, axis=1, keepdims=True)
        group = (2 * chip + (rank & 1)) * owners + owner
        lane = (me_wide * BLOCK + (rank >> 1)) & (LANES - 1)
        for half in range(2):
            part = slice(half * LANES, (half + 1) * LANES)
            group_ref[2 * n + half : 2 * n + half + 1, :] = group[:, part]
            lane_ref[2 * n + half : 2 * n + half + 1, :] = lane[:, part]


def places(cluster_ids, owners, peers):
    whole = pl.BlockSpec(memory_space=pltpu.VMEM)
    shape = jax.ShapeDtypeStruct((cluster_ids.shape[0] // LANES, LANES), jnp.int32)
    return pl.pallas_call(
        functools.partial(place_kernel, owners, peers),
        out_shape=(shape, shape),
        in_specs=[whole],
        out_specs=(whole, whole),
        compiler_params=pltpu.CompilerParams(vmem_limit_bytes=VMEM_LIMIT),
        name="places",
    )(cluster_ids.reshape(-1, LANES))


def in_block(owners, tile, length):
    place = tile * LANES + iota((owners, LANES), 1) - iota((owners, LANES), 0) * BLOCK
    return (place >= 0) & (place < length)


def keys_of(owners, rows_ref, meta_ref):
    for n in range(owners):
        last = n * BLOCK + SLOTS
        start = last // 16 * 16
        meta_ref[n : n + 1, :] = rows_ref[start : start + 16, :].astype(jnp.float32)[last - start : last - start + 1, :]
    meta = meta_ref[...]
    key = meta[:, :LANES] * 65536.0 + meta[:, LANES : 2 * LANES] * 256.0 + meta[:, 2 * LANES : 3 * LANES]
    flat = [
        jnp.sum(jnp.where(in_block(owners, tile, SLOTS), key, 0.0), axis=0, keepdims=True)
        for tile in range(rows_ref.shape[0] // LANES)
    ]
    over = jnp.max(meta[:, 3 * LANES : 3 * LANES + HALF])
    busiest = meta[:, 3 * LANES + HALF :]
    return flat, jnp.where(jnp.max(busiest) == jnp.min(busiest), over, 1.0)


def fold(rows_ref, key_rows_ref, keys, query_ref, best_in, best_ref):
    slots, width = rows_ref.shape
    for tile in range(0, slots // LANES, 2):
        scores = dot(rows_ref[tile * LANES : (tile + 2) * LANES, :], key_rows_ref[...], 1, 1)
        mine = jnp.concatenate([query_ref[:, tile : tile + 1], query_ref[:, tile + 1 : tile + 2]], axis=0)
        first = jnp.floor((mine - 1.0) * (1.0 / ORDER_SPAN)) * ORDER_SPAN
        allowed = (keys < mine) & (keys > first)
        best = jnp.max(jnp.where(allowed, scores, -float(width)), axis=1, keepdims=True) * (1.0 / width)
        best = jnp.maximum(best, -1.0)
        for half in range(2):
            part = best[half * LANES : (half + 1) * LANES]
            if best_in is not None:
                part = jnp.maximum(part, best_in[:, tile + half : tile + half + 1])
            best_ref[:, tile + half : tile + half + 1] = part


def own_kernel(owners, rows_ref, query_ref, best_ref, meta_ref):
    flat, _ = keys_of(owners, rows_ref, meta_ref)
    query_ref[...] = jnp.concatenate(
        flat + [jnp.zeros((LANES - len(flat), LANES), jnp.float32)], axis=0
    ).T
    fold(rows_ref, rows_ref, jnp.concatenate(flat, axis=1), query_ref, None, best_ref)


def other_kernel(owners, rows_ref, other_ref, query_ref, best_in, out_ref, meta_ref, best_ref):
    flat, over = keys_of(owners, other_ref, meta_ref)
    fold(rows_ref, other_ref, jnp.concatenate(flat, axis=1), query_ref, best_in, best_ref)
    turned = best_ref[...].T
    result = jnp.zeros((owners, LANES), jnp.float32)
    for tile in range(len(flat)):
        result = jnp.where(in_block(owners, tile, SLOTS), turned[tile : tile + 1, :], result)
        result = jnp.where(in_block(owners, tile, BLOCK) & ~in_block(owners, tile, SLOTS), over, result)
    out_ref[...] = result


def score(rows, owners):
    slots, width = rows.shape
    whole = pl.BlockSpec(memory_space=pltpu.VMEM)
    square = jax.ShapeDtypeStruct((LANES, LANES), jnp.float32)
    cost = pl.CostEstimate(
        flops=2 * slots * slots * width, bytes_accessed=4 * slots * width, transcendentals=0
    )
    peers = lax.axis_size("narrow")
    other = lax.ppermute(rows, "narrow", [(n, n ^ 1) for n in range(peers)])
    meta = pltpu.VMEM((owners, width), jnp.float32)
    params = pltpu.CompilerParams(vmem_limit_bytes=VMEM_LIMIT)
    query, best = pl.pallas_call(
        functools.partial(own_kernel, owners),
        out_shape=(square, square),
        in_specs=[whole],
        out_specs=(whole, whole),
        scratch_shapes=[meta],
        compiler_params=params,
        cost_estimate=cost,
        name="score_own",
    )(rows)
    return pl.pallas_call(
        functools.partial(other_kernel, owners),
        out_shape=jax.ShapeDtypeStruct((owners, LANES), jnp.float32),
        in_specs=[whole] * 4,
        out_specs=whole,
        scratch_shapes=[meta, pltpu.VMEM((LANES, LANES), jnp.float32)],
        compiler_params=params,
        cost_estimate=cost,
        name="score_other",
    )(rows, other, query, best)


def pick_kernel(values_ref, group_ref, lane_ref, out_ref, over_ref):
    me_wide = lax.axis_index("wide")
    groups = values_ref.shape[0]
    values = values_ref[...]
    marked = iota((groups, LANES), 1) == ((me_wide * BLOCK + SLOTS) & (LANES - 1))
    over_ref[0, 0] = jnp.max(jnp.where(marked, values, 0.0)).astype(jnp.int32)
    turned = values.T
    high = turned.astype(jnp.bfloat16)
    rest = turned - high.astype(jnp.float32)
    middle = rest.astype(jnp.bfloat16)
    low = (rest - middle.astype(jnp.float32)).astype(jnp.bfloat16)
    parts = jnp.concatenate([high, middle, low], axis=0)
    for n in range(group_ref.shape[0] // 2):
        one_hot = jnp.where(iota((groups, CHUNK), 0) == chunk_of(group_ref, n), 1.0, 0.0).astype(jnp.bfloat16)
        by_lane = dot(parts, one_hot, 1, 0)
        by_lane = by_lane[:LANES] + by_lane[LANES : 2 * LANES] + by_lane[2 * LANES :]
        here = iota((LANES, CHUNK), 0) == chunk_of(lane_ref, n)
        picked = jnp.sum(jnp.where(here, by_lane, 0.0), axis=0, keepdims=True)
        out_ref[2 * n : 2 * n + 1, :] = picked[:, :LANES]
        out_ref[2 * n + 1 : 2 * n + 2, :] = picked[:, LANES:]


def pick(values, group, lane):
    whole = pl.BlockSpec(memory_space=pltpu.VMEM)
    return pl.pallas_call(
        pick_kernel,
        out_shape=(
            jax.ShapeDtypeStruct(group.shape, jnp.float32),
            jax.ShapeDtypeStruct((1, 1), jnp.int32),
        ),
        in_specs=[whole, whole, whole],
        out_specs=(whole, pl.BlockSpec(memory_space=pltpu.SMEM)),
        compiler_params=pltpu.CompilerParams(vmem_limit_bytes=VMEM_LIMIT),
        name="pick",
    )(values, group, lane)


def unit_vectors(row_codes, row_scales, row_biases):
    values = row_codes.astype(jnp.float32) * row_scales[:, None] + row_biases[:, None]
    return (values * lax.rsqrt(jnp.mean(values * values, axis=1, keepdims=True) + epsilon)).astype(
        jnp.bfloat16
    )


def fold_block(
    queries, query_cluster, query_order, running, block_rows, block_cluster, block_order
):
    feature_width = queries.shape[-1]
    scores = (
        jnp.einsum("qe,ke->qk", queries, block_rows, preferred_element_type=jnp.float32)
        / feature_width
    )
    allowed = (query_cluster[:, None] == block_cluster[None, :]) & (
        block_order[None, :] < query_order[:, None]
    )
    return jnp.maximum(running, jnp.max(jnp.where(allowed, scores, -1.0), axis=1))


def fold_keys(
    queries, query_cluster, query_order, share_rows, running, piece_rows, piece_cluster, piece_order
):
    feature_width = piece_rows.shape[2]
    blocks = piece_rows.shape[1] // share_rows

    def visit_block(block_index, best_now):
        start_col = block_index * share_rows
        block_rows = lax.dynamic_slice_in_dim(piece_rows, start_col, share_rows, 1).reshape(
            -1, feature_width
        )
        block_cluster = lax.dynamic_slice_in_dim(piece_cluster, start_col, share_rows, 1).reshape(
            -1
        )
        block_order = lax.dynamic_slice_in_dim(piece_order, start_col, share_rows, 1).reshape(-1)
        return fold_block(
            queries, query_cluster, query_order, best_now, block_rows, block_cluster, block_order
        )

    return lax.fori_loop(0, blocks, visit_block, running)


def any_skew(row_codes, row_scales, row_biases, cluster_ids, order_index):
    owners = lax.axis_size("wide")
    peer_count = lax.axis_size("narrow")
    local_rows = row_codes.shape[0]
    feature_width = row_codes.shape[1]
    capacity = 2 * local_rows // owners
    share_rows = capacity // peer_count
    total_slots = owners * capacity
    unit_rows = unit_vectors(row_codes, row_scales, row_biases)
    owner_of = cluster_ids % owners
    one_hot = (owner_of[:, None] == jnp.arange(owners, dtype=jnp.int32)[None, :]).astype(jnp.int32)
    before = jnp.cumsum(one_hot, axis=0) - one_hot
    slot_rank = jnp.sum(before * one_hot, axis=1)
    slot_index = owner_of * capacity + slot_rank
    send_rows = jnp.zeros((total_slots, feature_width), jnp.bfloat16).at[slot_index].set(unit_rows)
    send_rows = send_rows.reshape(owners, capacity, feature_width)
    send_cluster = (
        jnp.full((total_slots,), -1, jnp.int32)
        .at[slot_index]
        .set(cluster_ids)
        .reshape(owners, capacity)
    )
    send_order = (
        jnp.full((total_slots,), -1, jnp.int32)
        .at[slot_index]
        .set(order_index)
        .reshape(owners, capacity)
    )
    offset = lax.axis_index("narrow") * share_rows
    initial = jnp.full((owners * share_rows,), -1.0, jnp.float32)
    got_rows, got_cluster, got_order = (
        lax.all_to_all(send_rows, "wide", split_axis=0, concat_axis=0, tiled=True),
        lax.all_to_all(send_cluster, "wide", split_axis=0, concat_axis=0, tiled=True),
        lax.all_to_all(send_order, "wide", split_axis=0, concat_axis=0, tiled=True),
    )
    queries = lax.dynamic_slice_in_dim(got_rows, offset, share_rows, 1).reshape(-1, feature_width)
    query_cluster = lax.dynamic_slice_in_dim(got_cluster, offset, share_rows, 1).reshape(-1)
    query_order = lax.dynamic_slice_in_dim(got_order, offset, share_rows, 1).reshape(-1)
    best_sim = fold_keys(
        queries, query_cluster, query_order, share_rows, initial, got_rows, got_cluster, got_order
    )
    column = lax.all_gather(best_sim.reshape(owners, share_rows), "narrow", axis=1, tiled=True)
    returned = lax.all_to_all(column, "wide", split_axis=0, concat_axis=0, tiled=True)
    return returned.reshape(-1)[slot_index]


def shards(row_codes, row_scales, row_biases, cluster_ids, order_index):
    owners = lax.axis_size("wide")
    peers = lax.axis_size("narrow")
    width = row_codes.shape[1]
    sent = pack(row_codes, row_scales, row_biases, cluster_ids, order_index, owners, peers)
    got = lax.all_to_all(
        sent.reshape(owners, BLOCK, width), "wide", split_axis=0, concat_axis=0, tiled=True
    ).reshape(owners * BLOCK, width)
    group, lane = places(cluster_ids, owners, peers)
    best = score(got, owners)
    back = lax.all_to_all(best.reshape(owners, 1, LANES), "wide", split_axis=0, concat_axis=0, tiled=True)
    copies = jnp.broadcast_to(back.reshape(1, owners, LANES), (peers, owners, LANES))
    values = lax.all_to_all(copies, "narrow", split_axis=0, concat_axis=0, tiled=True)
    values = values.reshape(peers * owners, LANES)
    picked, over = pick(values, group, lane)
    _, result = lax.while_loop(
        lambda state: state[0] > 0,
        lambda state: (
            jnp.zeros_like(state[0]),
            any_skew(row_codes, row_scales, row_biases, cluster_ids, order_index),
        ),
        (over[0, 0], picked.reshape(-1)),
    )
    return result


def solution(mesh):
    in_specs = (P("wide", None), P("wide"), P("wide"), P("wide"), P("wide"))
    out_specs = P("wide")
    return jax.shard_map(shards, mesh=mesh, in_specs=in_specs, out_specs=out_specs, check_vma=False)
```

```python
import functools

import jax
import jax.numpy as jnp
from jax import lax
from jax.experimental import pallas as pl
from jax.experimental.pallas import tpu as pltpu
from jax.sharding import PartitionSpec as P

epsilon = 1e-06

BLOCK = 32
SLOTS = BLOCK - 1
LANES = 128
HALF = LANES // 2
PITCH = 5
LENT_FIRST, LENT = 4, 8
HOST_CHIPS = -1620452551
TAKE = 4
CHUNK = 256
ORDER_SPAN = 131072
VMEM_LIMIT = 48 * 1024 * 1024


def iota(shape, axis):
    return lax.broadcasted_iota(jnp.int32, shape, axis)


def dot(left, right, left_axis, right_axis):
    return lax.dot_general(
        left, right, (((left_axis,), (right_axis,)), ((), ())), preferred_element_type=jnp.float32
    )


def strictly_before():
    return (iota((CHUNK, CHUNK), 0) < iota((CHUNK, CHUNK), 1)).astype(jnp.bfloat16)


def chunk_of(ref, index):
    return jnp.concatenate([ref[2 * index : 2 * index + 1, :], ref[2 * index + 1 : 2 * index + 2, :]], axis=1)


def split(clusters, owners):
    return clusters & (owners - 1), clusters >> (owners.bit_length() - 1)


def busiest_owner(cluster_ref, owners):
    total = jnp.zeros((owners, CHUNK), jnp.float32)
    for n in range(cluster_ref.shape[0] // 2):
        owner, _ = split(chunk_of(cluster_ref, n), owners)
        total = total + jnp.where(iota((owners, CHUNK), 0) == owner, 1.0, 0.0)
    total = jnp.sum(total, axis=1, keepdims=True)
    at_top = total == jnp.max(total, axis=0, keepdims=True)
    return jnp.min(jnp.where(at_top, iota((owners, 1), 0), owners), axis=0, keepdims=True)


def owner_place_chip(clusters, owners, peers, busiest):
    owner, place = split(clusters, owners)
    ahead = (owner - busiest) & (owners - 1)
    folded = jnp.minimum(place, 2 * peers - 1 - place)
    lent = (ahead == 0) & (place >= LENT_FIRST) & (place < LENT_FIRST + LENT)
    host_chip = lax.shift_right_logical(jnp.full_like(place, HOST_CHIPS), 2 * place) & 3
    chip = jnp.where(ahead <= LENT, host_chip, folded >> 1)
    chip = jnp.where(lent, 0, jnp.where(ahead == 0, folded & 3, chip))
    owner = jnp.where(lent, (owner + place + 1 - LENT_FIRST) & (owners - 1), owner)
    return owner, place, chip


def pack_kernel(
    owners, peers, cluster_ref, order_ref, scale_hbm, bias_hbm, codes_hbm, out_ref,
    codes_half, codes_full, slots_full, table_vmem, table_smem, scale_ref, bias_ref, code_sems, small_sems,
):
    local_rows = codes_hbm.shape[0]
    me_wide = lax.axis_index("wide")
    me_narrow = lax.axis_index("narrow")
    pieces = code_sems.shape[0]
    tiles = codes_hbm.shape[1] // LANES
    piece = local_rows // pieces
    copies = [
        pltpu.make_async_copy(
            codes_hbm.at[pl.ds(n * piece, piece)], codes_half.at[pl.ds(n * piece, piece)], code_sems.at[n]
        )
        for n in range(pieces)
    ]
    small_copies = [
        pltpu.make_async_copy(scale_hbm, scale_ref, small_sems.at[0]),
        pltpu.make_async_copy(bias_hbm, bias_ref, small_sems.at[1]),
    ]
    for copy in copies + small_copies:
        copy.start()

    chunks = local_rows // CHUNK
    busiest = busiest_owner(cluster_ref, owners)
    places, masks, hots = [], [], []
    for n in range(chunks):
        owner, place, chip = owner_place_chip(chunk_of(cluster_ref, n), owners, peers, busiest)
        mask = iota((owners, CHUNK), 0) == jnp.where(chip == me_narrow >> 1, owner, -1)
        places.append(place)
        masks.append(mask)
        hots.append(jnp.where(mask, 1.0, 0.0))
    earlier = dot(jnp.concatenate(hots, axis=0).astype(jnp.bfloat16), strictly_before(), 1, 0)
    count = jnp.zeros((owners, 1), jnp.float32)
    spread = []
    for n in range(chunks):
        within = earlier[n * owners : (n + 1) * owners]
        rank = jnp.sum(jnp.where(masks[n], within + count, 0.0), axis=0, keepdims=True).astype(jnp.int32)
        count = count + within[:, CHUNK - 1 :] + hots[n][:, CHUNK - 1 :]
        slot = jnp.where((rank & 1) == (me_narrow & 1), rank >> 1, -1)
        key = places[n] * ORDER_SPAN + chunk_of(order_ref, n) + 1
        row = n * CHUNK + iota((1, CHUNK), 1)
        at_slot = iota((BLOCK, CHUNK), 0) == slot
        parts = [
            jnp.where(at_slot, part.astype(jnp.float32), 0.0).astype(jnp.bfloat16)
            for part in (row >> 6, row & 63, key >> 16, (key >> 8) & 255, key & 255)
        ]
        spread.append(jnp.concatenate(parts, axis=0))
    table = dot(
        jnp.concatenate(spread, axis=1), jnp.concatenate(hots, axis=1).astype(jnp.bfloat16), 1, 1
    )
    rows_at = table[:BLOCK] * 64.0 + table[BLOCK : 2 * BLOCK]
    wide = jnp.concatenate([count, jnp.zeros((owners, LANES - 1), jnp.float32)], axis=1)
    counts = jnp.concatenate([wide, jnp.zeros((LANES - owners, LANES), jnp.float32)], axis=0).T[:1, :owners]
    used = jnp.minimum((counts.astype(jnp.int32) + 1 - (me_narrow & 1)) >> 1, SLOTS)
    table_vmem[:, :owners] = jnp.concatenate(
        [rows_at.astype(jnp.int32), jnp.broadcast_to(used, (8, owners))], axis=0
    )
    table_copy = pltpu.make_async_copy(table_vmem, table_smem, small_sems.at[2])
    table_copy.start()
    over = jnp.where(jnp.max(count) > 2 * SLOTS, 1.0, 0.0)
    turn = (me_wide * BLOCK) & (LANES - 1)
    meta = []
    for n in range(2, 5):
        part = jnp.concatenate(
            [table[n * BLOCK : n * BLOCK + SLOTS + 1], jnp.zeros((LANES - BLOCK, owners), jnp.float32)], axis=0
        )
        part = jnp.concatenate([part, jnp.zeros((LANES, LANES - owners), jnp.float32)], axis=1).T
        meta.append(pltpu.roll(part[:owners], turn, 1))
    lane = iota((owners, LANES), 1)
    meta.append(jnp.where(lane < HALF, over, busiest.astype(jnp.float32)))

    slots_full[...] = jnp.zeros_like(slots_full)
    for n, copy in enumerate(copies):
        copy.wait()
        values = codes_half[n * piece : (n + 1) * piece, :].astype(jnp.float32)
        for tile in range(tiles):
            codes_full[pl.ds(n * piece * PITCH + tile, piece, stride=PITCH), :] = values[
                :, tile * LANES : (tile + 1) * LANES
            ]
    for copy in [table_copy] + small_copies:
        copy.wait()

    def two_owners(half, carry):
        pair = (2 * half, 2 * half + 1)
        used = jnp.maximum(table_smem[BLOCK, pair[0]], table_smem[BLOCK, pair[1]])

        def eight_rows(group, carry):
            for owner in pair:
                for n in range(8):
                    slot = group * 8 + n
                    row = table_smem[slot, owner]
                    slots_full[pl.ds((owner * BLOCK + slot) * PITCH, TAKE), :] = (
                        codes_full[pl.ds(row * PITCH, TAKE), :] * scale_ref[row]
                        + bias_ref[row]
                    )
            return carry

        return lax.fori_loop(0, (used + 7) // 8, eight_rows, carry)

    lax.fori_loop(0, owners // 2, two_owners, 0)

    pair = 2 * BLOCK
    width = tiles * LANES
    for n in range(owners // 2):
        values = [
            slots_full[pl.ds(n * pair * PITCH + tile, pair, stride=PITCH), :] for tile in range(tiles)
        ]
        squares = functools.reduce(jnp.add, [value * value for value in values])
        mean_square = jnp.sum(squares, axis=1, keepdims=True) * (1.0 / width)
        factor = lax.rsqrt(mean_square + epsilon)
        place = iota((pair, 1), 0)
        for tile in range(tiles):
            unit = values[tile] * factor
            unit = jnp.where(place == SLOTS, meta[tile][2 * n : 2 * n + 1], unit)
            unit = jnp.where(place == BLOCK + SLOTS, meta[tile][2 * n + 1 : 2 * n + 2], unit)
            out_ref[n * pair : (n + 1) * pair, tile * LANES : (tile + 1) * LANES] = unit.astype(jnp.bfloat16)


def pack(row_codes, row_scales, row_biases, cluster_ids, order_index, owners, peers):
    local_rows, width = row_codes.shape
    whole = pl.BlockSpec(memory_space=pltpu.VMEM)
    outside = pl.BlockSpec(memory_space=pl.ANY)
    pieces = 8
    return pl.pallas_call(
        functools.partial(pack_kernel, owners, peers),
        out_shape=jax.ShapeDtypeStruct((owners * BLOCK, width), jnp.bfloat16),
        in_specs=[whole, whole, outside, outside, outside],
        out_specs=whole,
        scratch_shapes=[
            pltpu.VMEM((local_rows, width), jnp.bfloat16),
            pltpu.VMEM((local_rows * PITCH, LANES), jnp.float32),
            pltpu.VMEM((owners * BLOCK * PITCH, LANES), jnp.float32),
            pltpu.VMEM((BLOCK + 8, LANES), jnp.int32),
            pltpu.SMEM((BLOCK + 8, LANES), jnp.int32),
            pltpu.SMEM((local_rows,), jnp.float32),
            pltpu.SMEM((local_rows,), jnp.float32),
            pltpu.SemaphoreType.DMA((pieces,)),
            pltpu.SemaphoreType.DMA((3,)),
        ],
        compiler_params=pltpu.CompilerParams(vmem_limit_bytes=VMEM_LIMIT),
        name="pack",
    )(
        cluster_ids.reshape(-1, LANES), order_index.reshape(-1, LANES), row_scales, row_biases, row_codes,
    )


def place_kernel(owners, peers, cluster_ref, group_ref, slot_ref):
    groups = owners * peers // 2
    before = strictly_before()
    count = jnp.zeros((groups, 1), jnp.float32)
    busiest = busiest_owner(cluster_ref, owners)
    for n in range(cluster_ref.shape[0] // 2):
        owner, _, chip = owner_place_chip(chunk_of(cluster_ref, n), owners, peers, busiest)
        mine = iota((groups, CHUNK), 0) == chip * owners + owner
        one_hot = jnp.where(mine, 1.0, 0.0)
        earlier = dot(one_hot.astype(jnp.bfloat16), before, 1, 0) + count
        rank = jnp.sum(jnp.where(mine, earlier, 0.0), axis=0, keepdims=True).astype(jnp.int32)
        count = count + jnp.sum(one_hot, axis=1, keepdims=True)
        group = (2 * chip + (rank & 1)) * owners + owner
        slot = jnp.minimum(rank >> 1, SLOTS)
        for half in range(2):
            part = slice(half * LANES, (half + 1) * LANES)
            group_ref[2 * n + half : 2 * n + half + 1, :] = group[:, part]
            slot_ref[2 * n + half : 2 * n + half + 1, :] = slot[:, part]


def places(cluster_ids, owners, peers):
    whole = pl.BlockSpec(memory_space=pltpu.VMEM)
    shape = jax.ShapeDtypeStruct((cluster_ids.shape[0] // LANES, LANES), jnp.int32)
    return pl.pallas_call(
        functools.partial(place_kernel, owners, peers),
        out_shape=(shape, shape),
        in_specs=[whole],
        out_specs=(whole, whole),
        compiler_params=pltpu.CompilerParams(vmem_limit_bytes=VMEM_LIMIT),
        name="places",
    )(cluster_ids.reshape(-1, LANES))


def in_block(owners, tile, length):
    place = tile * LANES + iota((owners, LANES), 1) - iota((owners, LANES), 0) * BLOCK
    return (place >= 0) & (place < length)


def keys_of(owners, rows_ref, meta_ref):
    for n in range(owners):
        last = n * BLOCK + SLOTS
        start = last // 16 * 16
        meta_ref[n : n + 1, :] = rows_ref[start : start + 16, :].astype(jnp.float32)[last - start : last - start + 1, :]
    meta = meta_ref[...]
    key = meta[:, :LANES] * 65536.0 + meta[:, LANES : 2 * LANES] * 256.0 + meta[:, 2 * LANES : 3 * LANES]
    flat = [
        jnp.sum(jnp.where(in_block(owners, tile, SLOTS), key, 0.0), axis=0, keepdims=True)
        for tile in range(rows_ref.shape[0] // LANES)
    ]
    over = jnp.max(meta[:, 3 * LANES : 3 * LANES + HALF])
    busiest = meta[:, 3 * LANES + HALF :]
    return flat, jnp.where(jnp.max(busiest) == jnp.min(busiest), over, 1.0)


def fold(rows_ref, key_rows_ref, keys, query_ref, best_in, best_ref):
    slots, width = rows_ref.shape
    for tile in range(0, slots // LANES, 2):
        scores = dot(rows_ref[tile * LANES : (tile + 2) * LANES, :], key_rows_ref[...], 1, 1)
        mine = jnp.concatenate([query_ref[:, tile : tile + 1], query_ref[:, tile + 1 : tile + 2]], axis=0)
        first = jnp.floor((mine - 1.0) * (1.0 / ORDER_SPAN)) * ORDER_SPAN
        allowed = (keys < mine) & (keys > first)
        best = jnp.max(jnp.where(allowed, scores, -float(width)), axis=1, keepdims=True) * (1.0 / width)
        best = jnp.maximum(best, -1.0)
        for half in range(2):
            part = best[half * LANES : (half + 1) * LANES]
            if best_in is not None:
                part = jnp.maximum(part, best_in[:, tile + half : tile + half + 1])
            best_ref[:, tile + half : tile + half + 1] = part


def own_kernel(owners, rows_ref, query_ref, best_ref, meta_ref):
    flat, _ = keys_of(owners, rows_ref, meta_ref)
    query_ref[...] = jnp.concatenate(
        flat + [jnp.zeros((LANES - len(flat), LANES), jnp.float32)], axis=0
    ).T
    fold(rows_ref, rows_ref, jnp.concatenate(flat, axis=1), query_ref, None, best_ref)


def other_kernel(owners, rows_ref, other_ref, query_ref, best_in, out_ref, meta_ref, best_ref):
    flat, over = keys_of(owners, other_ref, meta_ref)
    fold(rows_ref, other_ref, jnp.concatenate(flat, axis=1), query_ref, best_in, best_ref)
    turned = best_ref[...].T
    result = jnp.zeros((owners, LANES), jnp.float32)
    for tile in range(len(flat)):
        result = jnp.where(in_block(owners, tile, SLOTS), turned[tile : tile + 1, :], result)
        result = jnp.where(in_block(owners, tile, BLOCK) & ~in_block(owners, tile, SLOTS), over, result)
    out_ref[...] = result


def score(rows, owners):
    slots, width = rows.shape
    whole = pl.BlockSpec(memory_space=pltpu.VMEM)
    square = jax.ShapeDtypeStruct((LANES, LANES), jnp.float32)
    cost = pl.CostEstimate(
        flops=2 * slots * slots * width, bytes_accessed=4 * slots * width, transcendentals=0
    )
    peers = lax.axis_size("narrow")
    other = lax.ppermute(rows, "narrow", [(n, n ^ 1) for n in range(peers)])
    meta = pltpu.VMEM((owners, width), jnp.float32)
    params = pltpu.CompilerParams(vmem_limit_bytes=VMEM_LIMIT)
    query, best = pl.pallas_call(
        functools.partial(own_kernel, owners),
        out_shape=(square, square),
        in_specs=[whole],
        out_specs=(whole, whole),
        scratch_shapes=[meta],
        compiler_params=params,
        cost_estimate=cost,
        name="score_own",
    )(rows)
    return pl.pallas_call(
        functools.partial(other_kernel, owners),
        out_shape=jax.ShapeDtypeStruct((owners, LANES), jnp.float32),
        in_specs=[whole] * 4,
        out_specs=whole,
        scratch_shapes=[meta, pltpu.VMEM((LANES, LANES), jnp.float32)],
        compiler_params=params,
        cost_estimate=cost,
        name="score_other",
    )(rows, other, query, best)


def pick_kernel(values_ref, group_ref, slot_ref, out_ref, over_ref):
    groups = values_ref.shape[0]
    turn = (lax.axis_index("wide") * BLOCK) & (LANES - 1)
    values = pltpu.roll(values_ref[...], (LANES - turn) & (LANES - 1), 1).T[:BLOCK]
    over_ref[0, 0] = jnp.max(values[SLOTS:]).astype(jnp.int32)
    high = values.astype(jnp.bfloat16)
    rest = values - high.astype(jnp.float32)
    middle = rest.astype(jnp.bfloat16)
    low = (rest - middle.astype(jnp.float32)).astype(jnp.bfloat16)
    parts = jnp.concatenate([high, middle, low], axis=0)
    for n in range(group_ref.shape[0] // 2):
        one_hot = jnp.where(iota((groups, CHUNK), 0) == chunk_of(group_ref, n), 1.0, 0.0).astype(jnp.bfloat16)
        by_slot = dot(parts, one_hot, 1, 0)
        by_slot = by_slot[:BLOCK] + by_slot[BLOCK : 2 * BLOCK] + by_slot[2 * BLOCK :]
        here = iota((BLOCK, CHUNK), 0) == chunk_of(slot_ref, n)
        picked = jnp.sum(jnp.where(here, by_slot, 0.0), axis=0, keepdims=True)
        out_ref[2 * n : 2 * n + 1, :] = picked[:, :LANES]
        out_ref[2 * n + 1 : 2 * n + 2, :] = picked[:, LANES:]


def pick(values, group, slot):
    whole = pl.BlockSpec(memory_space=pltpu.VMEM)
    return pl.pallas_call(
        pick_kernel,
        out_shape=(
            jax.ShapeDtypeStruct(group.shape, jnp.float32),
            jax.ShapeDtypeStruct((1, 1), jnp.int32),
        ),
        in_specs=[whole, whole, whole],
        out_specs=(whole, pl.BlockSpec(memory_space=pltpu.SMEM)),
        compiler_params=pltpu.CompilerParams(vmem_limit_bytes=VMEM_LIMIT),
        name="pick",
    )(values, group, slot)


def unit_vectors(row_codes, row_scales, row_biases):
    values = row_codes.astype(jnp.float32) * row_scales[:, None] + row_biases[:, None]
    return (values * lax.rsqrt(jnp.mean(values * values, axis=1, keepdims=True) + epsilon)).astype(
        jnp.bfloat16
    )


def fold_block(
    queries, query_cluster, query_order, running, block_rows, block_cluster, block_order
):
    feature_width = queries.shape[-1]
    scores = (
        jnp.einsum("qe,ke->qk", queries, block_rows, preferred_element_type=jnp.float32)
        / feature_width
    )
    allowed = (query_cluster[:, None] == block_cluster[None, :]) & (
        block_order[None, :] < query_order[:, None]
    )
    return jnp.maximum(running, jnp.max(jnp.where(allowed, scores, -1.0), axis=1))


def fold_keys(
    queries, query_cluster, query_order, share_rows, running, piece_rows, piece_cluster, piece_order
):
    feature_width = piece_rows.shape[2]
    blocks = piece_rows.shape[1] // share_rows

    def visit_block(block_index, best_now):
        start_col = block_index * share_rows
        block_rows = lax.dynamic_slice_in_dim(piece_rows, start_col, share_rows, 1).reshape(
            -1, feature_width
        )
        block_cluster = lax.dynamic_slice_in_dim(piece_cluster, start_col, share_rows, 1).reshape(
            -1
        )
        block_order = lax.dynamic_slice_in_dim(piece_order, start_col, share_rows, 1).reshape(-1)
        return fold_block(
            queries, query_cluster, query_order, best_now, block_rows, block_cluster, block_order
        )

    return lax.fori_loop(0, blocks, visit_block, running)


def any_skew(row_codes, row_scales, row_biases, cluster_ids, order_index):
    owners = lax.axis_size("wide")
    peer_count = lax.axis_size("narrow")
    local_rows = row_codes.shape[0]
    feature_width = row_codes.shape[1]
    capacity = 2 * local_rows // owners
    share_rows = capacity // peer_count
    total_slots = owners * capacity
    unit_rows = unit_vectors(row_codes, row_scales, row_biases)
    owner_of = cluster_ids % owners
    one_hot = (owner_of[:, None] == jnp.arange(owners, dtype=jnp.int32)[None, :]).astype(jnp.int32)
    before = jnp.cumsum(one_hot, axis=0) - one_hot
    slot_rank = jnp.sum(before * one_hot, axis=1)
    slot_index = owner_of * capacity + slot_rank
    send_rows = jnp.zeros((total_slots, feature_width), jnp.bfloat16).at[slot_index].set(unit_rows)
    send_rows = send_rows.reshape(owners, capacity, feature_width)
    send_cluster = (
        jnp.full((total_slots,), -1, jnp.int32)
        .at[slot_index]
        .set(cluster_ids)
        .reshape(owners, capacity)
    )
    send_order = (
        jnp.full((total_slots,), -1, jnp.int32)
        .at[slot_index]
        .set(order_index)
        .reshape(owners, capacity)
    )
    offset = lax.axis_index("narrow") * share_rows
    initial = jnp.full((owners * share_rows,), -1.0, jnp.float32)
    got_rows, got_cluster, got_order = (
        lax.all_to_all(send_rows, "wide", split_axis=0, concat_axis=0, tiled=True),
        lax.all_to_all(send_cluster, "wide", split_axis=0, concat_axis=0, tiled=True),
        lax.all_to_all(send_order, "wide", split_axis=0, concat_axis=0, tiled=True),
    )
    queries = lax.dynamic_slice_in_dim(got_rows, offset, share_rows, 1).reshape(-1, feature_width)
    query_cluster = lax.dynamic_slice_in_dim(got_cluster, offset, share_rows, 1).reshape(-1)
    query_order = lax.dynamic_slice_in_dim(got_order, offset, share_rows, 1).reshape(-1)
    best_sim = fold_keys(
        queries, query_cluster, query_order, share_rows, initial, got_rows, got_cluster, got_order
    )
    column = lax.all_gather(best_sim.reshape(owners, share_rows), "narrow", axis=1, tiled=True)
    returned = lax.all_to_all(column, "wide", split_axis=0, concat_axis=0, tiled=True)
    return returned.reshape(-1)[slot_index]


def shards(row_codes, row_scales, row_biases, cluster_ids, order_index):
    owners = lax.axis_size("wide")
    peers = lax.axis_size("narrow")
    width = row_codes.shape[1]
    sent = pack(row_codes, row_scales, row_biases, cluster_ids, order_index, owners, peers)
    got = lax.all_to_all(
        sent.reshape(owners, BLOCK, width), "wide", split_axis=0, concat_axis=0, tiled=True
    ).reshape(owners * BLOCK, width)
    group, slot = places(cluster_ids, owners, peers)
    best = score(got, owners)
    back = lax.all_to_all(best.reshape(owners, 1, LANES), "wide", split_axis=0, concat_axis=0, tiled=True)
    copies = jnp.broadcast_to(back.reshape(1, owners, LANES), (peers, owners, LANES))
    values = lax.all_to_all(copies, "narrow", split_axis=0, concat_axis=0, tiled=True)
    values = values.reshape(peers * owners, LANES)
    picked, over = pick(values, group, slot)
    _, result = lax.while_loop(
        lambda state: state[0] > 0,
        lambda state: (
            jnp.zeros_like(state[0]),
            any_skew(row_codes, row_scales, row_biases, cluster_ids, order_index),
        ),
        (over[0, 0], picked.reshape(-1)),
    )
    return result


def solution(mesh):
    in_specs = (P("wide", None), P("wide"), P("wide"), P("wide"), P("wide"))
    out_specs = P("wide")
    return jax.shard_map(shards, mesh=mesh, in_specs=in_specs, out_specs=out_specs, check_vma=False)
```

```python
import functools

import jax
import jax.numpy as jnp
from jax import lax
from jax.experimental import pallas as pl
from jax.experimental.pallas import tpu as pltpu
from jax.sharding import PartitionSpec as P

epsilon = 1e-06

BLOCK = 32
SLOTS = BLOCK - 1
LANES = 128
HALF = LANES // 2
PITCH = 5
LENT_FIRST, LENT = 4, 8
HOST_CHIPS = -1620452551
TAKE = 4
CHUNK = 256
ORDER_SPAN = 131072
VMEM_LIMIT = 48 * 1024 * 1024


def iota(shape, axis):
    return lax.broadcasted_iota(jnp.int32, shape, axis)


def dot(left, right, left_axis, right_axis):
    return lax.dot_general(
        left, right, (((left_axis,), (right_axis,)), ((), ())), preferred_element_type=jnp.float32
    )


def strictly_before():
    return (iota((CHUNK, CHUNK), 0) < iota((CHUNK, CHUNK), 1)).astype(jnp.bfloat16)


def chunk_of(ref, index):
    return jnp.concatenate([ref[2 * index : 2 * index + 1, :], ref[2 * index + 1 : 2 * index + 2, :]], axis=1)


def split(clusters, owners):
    return clusters & (owners - 1), clusters >> (owners.bit_length() - 1)


def busiest_owner(cluster_ref, owners):
    total = jnp.zeros((owners, CHUNK), jnp.float32)
    for n in range(cluster_ref.shape[0] // 2):
        owner, _ = split(chunk_of(cluster_ref, n), owners)
        total = total + jnp.where(iota((owners, CHUNK), 0) == owner, 1.0, 0.0)
    total = jnp.sum(total, axis=1, keepdims=True)
    at_top = total == jnp.max(total, axis=0, keepdims=True)
    return jnp.min(jnp.where(at_top, iota((owners, 1), 0), owners), axis=0, keepdims=True)


def owner_place_chip(clusters, owners, peers, busiest):
    owner, place = split(clusters, owners)
    ahead = (owner - busiest) & (owners - 1)
    folded = jnp.minimum(place, 2 * peers - 1 - place)
    lent = (ahead == 0) & (place >= LENT_FIRST) & (place < LENT_FIRST + LENT)
    host_chip = lax.shift_right_logical(jnp.full_like(place, HOST_CHIPS), 2 * place) & 3
    chip = jnp.where(ahead <= LENT, host_chip, folded >> 1)
    chip = jnp.where(lent, 0, jnp.where(ahead == 0, folded & 3, chip))
    owner = jnp.where(lent, (owner + place + 1 - LENT_FIRST) & (owners - 1), owner)
    return owner, place, chip


def pack_kernel(
    owners, peers, cluster_ref, order_ref, scale_hbm, bias_hbm, codes_hbm, out_ref, kept_ref,
    codes_half, codes_full, slots_full, table_vmem, table_smem, scale_ref, bias_ref, code_sems, small_sems,
):
    local_rows = codes_hbm.shape[0]
    me_wide = lax.axis_index("wide")
    me_narrow = lax.axis_index("narrow")
    pieces = code_sems.shape[0]
    tiles = codes_hbm.shape[1] // LANES
    piece = local_rows // pieces
    copies = [
        pltpu.make_async_copy(
            codes_hbm.at[pl.ds(n * piece, piece)], codes_half.at[pl.ds(n * piece, piece)], code_sems.at[n]
        )
        for n in range(pieces)
    ]
    small_copies = [
        pltpu.make_async_copy(scale_hbm, scale_ref, small_sems.at[0]),
        pltpu.make_async_copy(bias_hbm, bias_ref, small_sems.at[1]),
    ]
    for copy in copies + small_copies:
        copy.start()

    chunks = local_rows // CHUNK
    kept_ref[...] = cluster_ref[...]
    busiest = busiest_owner(cluster_ref, owners)
    places, masks, hots = [], [], []
    for n in range(chunks):
        owner, place, chip = owner_place_chip(chunk_of(cluster_ref, n), owners, peers, busiest)
        mask = iota((owners, CHUNK), 0) == jnp.where(chip == me_narrow >> 1, owner, -1)
        places.append(place)
        masks.append(mask)
        hots.append(jnp.where(mask, 1.0, 0.0))
    earlier = dot(jnp.concatenate(hots, axis=0).astype(jnp.bfloat16), strictly_before(), 1, 0)
    count = jnp.zeros((owners, 1), jnp.float32)
    spread = []
    for n in range(chunks):
        within = earlier[n * owners : (n + 1) * owners]
        rank = jnp.sum(jnp.where(masks[n], within + count, 0.0), axis=0, keepdims=True).astype(jnp.int32)
        count = count + within[:, CHUNK - 1 :] + hots[n][:, CHUNK - 1 :]
        slot = jnp.where((rank & 1) == (me_narrow & 1), rank >> 1, -1)
        key = places[n] * ORDER_SPAN + chunk_of(order_ref, n) + 1
        row = n * CHUNK + iota((1, CHUNK), 1)
        at_slot = iota((BLOCK, CHUNK), 0) == slot
        parts = [
            jnp.where(at_slot, part.astype(jnp.float32), 0.0).astype(jnp.bfloat16)
            for part in (row >> 6, row & 63, key >> 16, (key >> 8) & 255, key & 255)
        ]
        spread.append(jnp.concatenate(parts, axis=0))
    table = dot(
        jnp.concatenate(spread, axis=1), jnp.concatenate(hots, axis=1).astype(jnp.bfloat16), 1, 1
    )
    rows_at = table[:BLOCK] * 64.0 + table[BLOCK : 2 * BLOCK]
    wide = jnp.concatenate([count, jnp.zeros((owners, LANES - 1), jnp.float32)], axis=1)
    counts = jnp.concatenate([wide, jnp.zeros((LANES - owners, LANES), jnp.float32)], axis=0).T[:1, :owners]
    used = jnp.minimum((counts.astype(jnp.int32) + 1 - (me_narrow & 1)) >> 1, SLOTS)
    table_vmem[:, :owners] = jnp.concatenate(
        [rows_at.astype(jnp.int32), jnp.broadcast_to(used, (8, owners))], axis=0
    )
    table_copy = pltpu.make_async_copy(table_vmem, table_smem, small_sems.at[2])
    table_copy.start()
    over = jnp.where(jnp.max(count) > 2 * SLOTS, 1.0, 0.0)
    turn = (me_wide * BLOCK) & (LANES - 1)
    meta = []
    for n in range(2, 5):
        part = jnp.concatenate(
            [table[n * BLOCK : n * BLOCK + SLOTS + 1], jnp.zeros((LANES - BLOCK, owners), jnp.float32)], axis=0
        )
        part = jnp.concatenate([part, jnp.zeros((LANES, LANES - owners), jnp.float32)], axis=1).T
        meta.append(pltpu.roll(part[:owners], turn, 1))
    lane = iota((owners, LANES), 1)
    meta.append(jnp.where(lane < HALF, over, busiest.astype(jnp.float32)))

    slots_full[...] = jnp.zeros_like(slots_full)
    for n, copy in enumerate(copies):
        copy.wait()
        values = codes_half[n * piece : (n + 1) * piece, :].astype(jnp.float32)
        for tile in range(tiles):
            codes_full[pl.ds(n * piece * PITCH + tile, piece, stride=PITCH), :] = values[
                :, tile * LANES : (tile + 1) * LANES
            ]
    for copy in [table_copy] + small_copies:
        copy.wait()

    def two_owners(half, carry):
        pair = (2 * half, 2 * half + 1)
        used = jnp.maximum(table_smem[BLOCK, pair[0]], table_smem[BLOCK, pair[1]])

        def eight_rows(group, carry):
            for owner in pair:
                for n in range(8):
                    slot = group * 8 + n
                    row = table_smem[slot, owner]
                    slots_full[pl.ds((owner * BLOCK + slot) * PITCH, TAKE), :] = (
                        codes_full[pl.ds(row * PITCH, TAKE), :] * scale_ref[row]
                        + bias_ref[row]
                    )
            return carry

        return lax.fori_loop(0, (used + 7) // 8, eight_rows, carry)

    lax.fori_loop(0, owners // 2, two_owners, 0)

    pair = 2 * BLOCK
    width = tiles * LANES
    for n in range(owners // 2):
        values = [
            slots_full[pl.ds(n * pair * PITCH + tile, pair, stride=PITCH), :] for tile in range(tiles)
        ]
        squares = functools.reduce(jnp.add, [value * value for value in values])
        mean_square = jnp.sum(squares, axis=1, keepdims=True) * (1.0 / width)
        factor = lax.rsqrt(mean_square + epsilon)
        place = iota((pair, 1), 0)
        for tile in range(tiles):
            unit = values[tile] * factor
            unit = jnp.where(place == SLOTS, meta[tile][2 * n : 2 * n + 1], unit)
            unit = jnp.where(place == BLOCK + SLOTS, meta[tile][2 * n + 1 : 2 * n + 2], unit)
            out_ref[n * pair : (n + 1) * pair, tile * LANES : (tile + 1) * LANES] = unit.astype(jnp.bfloat16)


def pack(row_codes, row_scales, row_biases, cluster_ids, order_index, owners, peers):
    local_rows, width = row_codes.shape
    whole = pl.BlockSpec(memory_space=pltpu.VMEM)
    outside = pl.BlockSpec(memory_space=pl.ANY)
    pieces = 8
    return pl.pallas_call(
        functools.partial(pack_kernel, owners, peers),
        out_shape=(
            jax.ShapeDtypeStruct((owners * BLOCK, width), jnp.bfloat16),
            jax.ShapeDtypeStruct((local_rows // LANES, LANES), jnp.int32),
        ),
        in_specs=[whole, whole, outside, outside, outside],
        out_specs=(whole, whole),
        scratch_shapes=[
            pltpu.VMEM((local_rows, width), jnp.bfloat16),
            pltpu.VMEM((local_rows * PITCH, LANES), jnp.float32),
            pltpu.VMEM((owners * BLOCK * PITCH, LANES), jnp.float32),
            pltpu.VMEM((BLOCK + 8, LANES), jnp.int32),
            pltpu.SMEM((BLOCK + 8, LANES), jnp.int32),
            pltpu.SMEM((local_rows,), jnp.float32),
            pltpu.SMEM((local_rows,), jnp.float32),
            pltpu.SemaphoreType.DMA((pieces,)),
            pltpu.SemaphoreType.DMA((3,)),
        ],
        compiler_params=pltpu.CompilerParams(vmem_limit_bytes=VMEM_LIMIT),
        name="pack",
    )(
        cluster_ids.reshape(-1, LANES), order_index.reshape(-1, LANES), row_scales, row_biases, row_codes,
    )


def place_kernel(owners, peers, cluster_ref, group_ref, slot_ref):
    groups = owners * peers // 2
    before = strictly_before()
    count = jnp.zeros((groups, 1), jnp.float32)
    busiest = busiest_owner(cluster_ref, owners)
    for n in range(cluster_ref.shape[0] // 2):
        owner, _, chip = owner_place_chip(chunk_of(cluster_ref, n), owners, peers, busiest)
        mine = iota((groups, CHUNK), 0) == chip * owners + owner
        one_hot = jnp.where(mine, 1.0, 0.0)
        earlier = dot(one_hot.astype(jnp.bfloat16), before, 1, 0) + count
        rank = jnp.sum(jnp.where(mine, earlier, 0.0), axis=0, keepdims=True).astype(jnp.int32)
        count = count + jnp.sum(one_hot, axis=1, keepdims=True)
        peer = 2 * chip + (rank & 1)
        group = ((owner >> 3) * peers + peer) * 8 + (owner & 7)
        slot = jnp.minimum(rank >> 1, SLOTS)
        for half in range(2):
            part = slice(half * LANES, (half + 1) * LANES)
            group_ref[2 * n + half : 2 * n + half + 1, :] = group[:, part]
            slot_ref[2 * n + half : 2 * n + half + 1, :] = slot[:, part]


def places(clusters, owners, peers):
    whole = pl.BlockSpec(memory_space=pltpu.VMEM)
    shape = jax.ShapeDtypeStruct(clusters.shape, jnp.int32)
    return pl.pallas_call(
        functools.partial(place_kernel, owners, peers),
        out_shape=(shape, shape),
        in_specs=[whole],
        out_specs=(whole, whole),
        compiler_params=pltpu.CompilerParams(vmem_limit_bytes=VMEM_LIMIT),
        cost_estimate=pl.CostEstimate(flops=2**30, bytes_accessed=2**16, transcendentals=0),
        name="places",
    )(clusters)


def in_block(owners, tile, length):
    place = tile * LANES + iota((owners, LANES), 1) - iota((owners, LANES), 0) * BLOCK
    return (place >= 0) & (place < length)


def keys_of(owners, rows_ref, meta_ref):
    for n in range(owners):
        last = n * BLOCK + SLOTS
        start = last // 16 * 16
        meta_ref[n : n + 1, :] = rows_ref[start : start + 16, :].astype(jnp.float32)[last - start : last - start + 1, :]
    meta = meta_ref[...]
    key = meta[:, :LANES] * 65536.0 + meta[:, LANES : 2 * LANES] * 256.0 + meta[:, 2 * LANES : 3 * LANES]
    flat = [
        jnp.sum(jnp.where(in_block(owners, tile, SLOTS), key, 0.0), axis=0, keepdims=True)
        for tile in range(rows_ref.shape[0] // LANES)
    ]
    over = jnp.max(meta[:, 3 * LANES : 3 * LANES + HALF])
    busiest = meta[:, 3 * LANES + HALF :]
    return flat, jnp.where(jnp.max(busiest) == jnp.min(busiest), over, 1.0)


def fold(rows_ref, key_rows_ref, keys, query_ref, best_in, best_ref):
    slots, width = rows_ref.shape
    for tile in range(0, slots // LANES, 2):
        scores = dot(rows_ref[tile * LANES : (tile + 2) * LANES, :], key_rows_ref[...], 1, 1)
        mine = jnp.concatenate([query_ref[:, tile : tile + 1], query_ref[:, tile + 1 : tile + 2]], axis=0)
        first = jnp.floor((mine - 1.0) * (1.0 / ORDER_SPAN)) * ORDER_SPAN
        allowed = (keys < mine) & (keys > first)
        best = jnp.max(jnp.where(allowed, scores, -float(width)), axis=1, keepdims=True) * (1.0 / width)
        best = jnp.maximum(best, -1.0)
        for half in range(2):
            part = best[half * LANES : (half + 1) * LANES]
            if best_in is not None:
                part = jnp.maximum(part, best_in[:, tile + half : tile + half + 1])
            best_ref[:, tile + half : tile + half + 1] = part


def own_kernel(owners, rows_ref, query_ref, best_ref, meta_ref):
    flat, _ = keys_of(owners, rows_ref, meta_ref)
    query_ref[...] = jnp.concatenate(
        flat + [jnp.zeros((LANES - len(flat), LANES), jnp.float32)], axis=0
    ).T
    fold(rows_ref, rows_ref, jnp.concatenate(flat, axis=1), query_ref, None, best_ref)


def other_kernel(owners, rows_ref, other_ref, query_ref, best_in, out_ref, meta_ref, best_ref):
    flat, over = keys_of(owners, other_ref, meta_ref)
    fold(rows_ref, other_ref, jnp.concatenate(flat, axis=1), query_ref, best_in, best_ref)
    turned = best_ref[...].T
    result = jnp.zeros((owners, LANES), jnp.float32)
    for tile in range(len(flat)):
        result = jnp.where(in_block(owners, tile, SLOTS), turned[tile : tile + 1, :], result)
        result = jnp.where(in_block(owners, tile, BLOCK) & ~in_block(owners, tile, SLOTS), over, result)
    out_ref[...] = result


def score(rows, clusters, owners):
    slots, width = rows.shape
    whole = pl.BlockSpec(memory_space=pltpu.VMEM)
    square = jax.ShapeDtypeStruct((LANES, LANES), jnp.float32)
    cost = pl.CostEstimate(
        flops=2 * slots * slots * width, bytes_accessed=4 * slots * width, transcendentals=0
    )
    peers = lax.axis_size("narrow")
    other = lax.ppermute(rows, "narrow", [(n, n ^ 1) for n in range(peers)])
    meta = pltpu.VMEM((owners, width), jnp.float32)
    params = pltpu.CompilerParams(vmem_limit_bytes=VMEM_LIMIT)
    query, best = pl.pallas_call(
        functools.partial(own_kernel, owners),
        out_shape=(square, square),
        in_specs=[whole],
        out_specs=(whole, whole),
        scratch_shapes=[meta],
        compiler_params=params,
        cost_estimate=cost,
        name="score_own",
    )(rows)
    group, slot = places(clusters, owners, peers)
    other, query, best, group, slot = lax.optimization_barrier((other, query, best, group, slot))
    result = pl.pallas_call(
        functools.partial(other_kernel, owners),
        out_shape=jax.ShapeDtypeStruct((owners, LANES), jnp.float32),
        in_specs=[whole] * 4,
        out_specs=whole,
        scratch_shapes=[meta, pltpu.VMEM((LANES, LANES), jnp.float32)],
        compiler_params=params,
        cost_estimate=cost,
        name="score_other",
    )(rows, other, query, best)
    return result, group, slot


def spread_kernel(back_ref, out_ref):
    turn = (lax.axis_index("wide") * BLOCK) & (LANES - 1)
    lane = iota((8, LANES), 1) // BLOCK
    dense = jnp.zeros((8, LANES), jnp.float32)
    for n in range(LANES // BLOCK):
        part = pltpu.roll(back_ref[8 * n : 8 * n + 8, :], (n * BLOCK + LANES - turn) & (LANES - 1), 1)
        dense = jnp.where(lane == n, part, dense)
    for n in range(out_ref.shape[0]):
        out_ref[n] = dense


def spread(back, peers):
    whole = pl.BlockSpec(memory_space=pltpu.VMEM)
    return pl.pallas_call(
        spread_kernel,
        out_shape=jax.ShapeDtypeStruct((peers, 8, LANES), jnp.float32),
        in_specs=[whole],
        out_specs=whole,
        compiler_params=pltpu.CompilerParams(vmem_limit_bytes=VMEM_LIMIT),
        name="spread",
    )(back)


def pick_kernel(values_ref, group_ref, slot_ref, out_ref, over_ref):
    turned = values_ref[...].T
    values = jnp.concatenate(
        [turned[n * BLOCK : (n + 1) * BLOCK] for n in range(LANES // BLOCK)], axis=1
    )
    groups = values.shape[1]
    over_ref[0, 0] = jnp.max(values[SLOTS:]).astype(jnp.int32)
    high = values.astype(jnp.bfloat16)
    rest = values - high.astype(jnp.float32)
    middle = rest.astype(jnp.bfloat16)
    low = (rest - middle.astype(jnp.float32)).astype(jnp.bfloat16)
    parts = jnp.concatenate([high, middle, low], axis=0)
    for n in range(group_ref.shape[0] // 2):
        one_hot = jnp.where(iota((groups, CHUNK), 0) == chunk_of(group_ref, n), 1.0, 0.0).astype(jnp.bfloat16)
        by_slot = dot(parts, one_hot, 1, 0)
        by_slot = by_slot[:BLOCK] + by_slot[BLOCK : 2 * BLOCK] + by_slot[2 * BLOCK :]
        here = iota((BLOCK, CHUNK), 0) == chunk_of(slot_ref, n)
        picked = jnp.sum(jnp.where(here, by_slot, 0.0), axis=0, keepdims=True)
        out_ref[2 * n : 2 * n + 1, :] = picked[:, :LANES]
        out_ref[2 * n + 1 : 2 * n + 2, :] = picked[:, LANES:]


def pick(values, group, slot):
    whole = pl.BlockSpec(memory_space=pltpu.VMEM)
    return pl.pallas_call(
        pick_kernel,
        out_shape=(
            jax.ShapeDtypeStruct(group.shape, jnp.float32),
            jax.ShapeDtypeStruct((1, 1), jnp.int32),
        ),
        in_specs=[whole, whole, whole],
        out_specs=(whole, pl.BlockSpec(memory_space=pltpu.SMEM)),
        compiler_params=pltpu.CompilerParams(vmem_limit_bytes=VMEM_LIMIT),
        name="pick",
    )(values, group, slot)


def unit_vectors(row_codes, row_scales, row_biases):
    values = row_codes.astype(jnp.float32) * row_scales[:, None] + row_biases[:, None]
    return (values * lax.rsqrt(jnp.mean(values * values, axis=1, keepdims=True) + epsilon)).astype(
        jnp.bfloat16
    )


def fold_block(
    queries, query_cluster, query_order, running, block_rows, block_cluster, block_order
):
    feature_width = queries.shape[-1]
    scores = (
        jnp.einsum("qe,ke->qk", queries, block_rows, preferred_element_type=jnp.float32)
        / feature_width
    )
    allowed = (query_cluster[:, None] == block_cluster[None, :]) & (
        block_order[None, :] < query_order[:, None]
    )
    return jnp.maximum(running, jnp.max(jnp.where(allowed, scores, -1.0), axis=1))


def fold_keys(
    queries, query_cluster, query_order, share_rows, running, piece_rows, piece_cluster, piece_order
):
    feature_width = piece_rows.shape[2]
    blocks = piece_rows.shape[1] // share_rows

    def visit_block(block_index, best_now):
        start_col = block_index * share_rows
        block_rows = lax.dynamic_slice_in_dim(piece_rows, start_col, share_rows, 1).reshape(
            -1, feature_width
        )
        block_cluster = lax.dynamic_slice_in_dim(piece_cluster, start_col, share_rows, 1).reshape(
            -1
        )
        block_order = lax.dynamic_slice_in_dim(piece_order, start_col, share_rows, 1).reshape(-1)
        return fold_block(
            queries, query_cluster, query_order, best_now, block_rows, block_cluster, block_order
        )

    return lax.fori_loop(0, blocks, visit_block, running)


def any_skew(row_codes, row_scales, row_biases, cluster_ids, order_index):
    owners = lax.axis_size("wide")
    peer_count = lax.axis_size("narrow")
    local_rows = row_codes.shape[0]
    feature_width = row_codes.shape[1]
    capacity = 2 * local_rows // owners
    share_rows = capacity // peer_count
    total_slots = owners * capacity
    unit_rows = unit_vectors(row_codes, row_scales, row_biases)
    owner_of = cluster_ids % owners
    one_hot = (owner_of[:, None] == jnp.arange(owners, dtype=jnp.int32)[None, :]).astype(jnp.int32)
    before = jnp.cumsum(one_hot, axis=0) - one_hot
    slot_rank = jnp.sum(before * one_hot, axis=1)
    slot_index = owner_of * capacity + slot_rank
    send_rows = jnp.zeros((total_slots, feature_width), jnp.bfloat16).at[slot_index].set(unit_rows)
    send_rows = send_rows.reshape(owners, capacity, feature_width)
    send_cluster = (
        jnp.full((total_slots,), -1, jnp.int32)
        .at[slot_index]
        .set(cluster_ids)
        .reshape(owners, capacity)
    )
    send_order = (
        jnp.full((total_slots,), -1, jnp.int32)
        .at[slot_index]
        .set(order_index)
        .reshape(owners, capacity)
    )
    offset = lax.axis_index("narrow") * share_rows
    initial = jnp.full((owners * share_rows,), -1.0, jnp.float32)
    got_rows, got_cluster, got_order = (
        lax.all_to_all(send_rows, "wide", split_axis=0, concat_axis=0, tiled=True),
        lax.all_to_all(send_cluster, "wide", split_axis=0, concat_axis=0, tiled=True),
        lax.all_to_all(send_order, "wide", split_axis=0, concat_axis=0, tiled=True),
    )
    queries = lax.dynamic_slice_in_dim(got_rows, offset, share_rows, 1).reshape(-1, feature_width)
    query_cluster = lax.dynamic_slice_in_dim(got_cluster, offset, share_rows, 1).reshape(-1)
    query_order = lax.dynamic_slice_in_dim(got_order, offset, share_rows, 1).reshape(-1)
    best_sim = fold_keys(
        queries, query_cluster, query_order, share_rows, initial, got_rows, got_cluster, got_order
    )
    column = lax.all_gather(best_sim.reshape(owners, share_rows), "narrow", axis=1, tiled=True)
    returned = lax.all_to_all(column, "wide", split_axis=0, concat_axis=0, tiled=True)
    return returned.reshape(-1)[slot_index]


def shards(row_codes, row_scales, row_biases, cluster_ids, order_index):
    owners = lax.axis_size("wide")
    peers = lax.axis_size("narrow")
    width = row_codes.shape[1]
    sent, clusters = pack(row_codes, row_scales, row_biases, cluster_ids, order_index, owners, peers)
    got = lax.all_to_all(
        sent.reshape(owners, BLOCK, width), "wide", split_axis=0, concat_axis=0, tiled=True
    ).reshape(owners * BLOCK, width)
    best, group, slot = score(got, clusters, owners)
    back = lax.all_to_all(best.reshape(owners, 1, LANES), "wide", split_axis=0, concat_axis=0, tiled=True)
    copies = spread(back.reshape(owners, LANES), peers)
    values = lax.all_to_all(copies, "narrow", split_axis=0, concat_axis=0, tiled=True)
    values = values.reshape(peers * 8, LANES)
    picked, over = pick(values, group, slot)
    _, result = lax.while_loop(
        lambda state: state[0] > 0,
        lambda state: (
            jnp.zeros_like(state[0]),
            any_skew(row_codes, row_scales, row_biases, cluster_ids, order_index),
        ),
        (over[0, 0], picked.reshape(-1)),
    )
    return result


def solution(mesh):
    in_specs = (P("wide", None), P("wide"), P("wide"), P("wide"), P("wide"))
    out_specs = P("wide")
    return jax.shard_map(shards, mesh=mesh, in_specs=in_specs, out_specs=out_specs, check_vma=False)
```

```python
import functools

import jax
import jax.numpy as jnp
from jax import lax
from jax.experimental import pallas as pl
from jax.experimental.pallas import tpu as pltpu
from jax.sharding import PartitionSpec as P

epsilon = 1e-06

BLOCK = 32
SLOTS = BLOCK - 1
LANES = 128
HALF = LANES // 2
PITCH = 5
LENT_FIRST, LENT = 4, 8
HOST_CHIPS = -1620452551
TAKE = 4
CHUNK = 256
ORDER_SPAN = 131072
VMEM_LIMIT = 48 * 1024 * 1024


def iota(shape, axis):
    return lax.broadcasted_iota(jnp.int32, shape, axis)


def dot(left, right, left_axis, right_axis):
    return lax.dot_general(
        left, right, (((left_axis,), (right_axis,)), ((), ())), preferred_element_type=jnp.float32
    )


def strictly_before():
    return (iota((CHUNK, CHUNK), 0) < iota((CHUNK, CHUNK), 1)).astype(jnp.bfloat16)


def chunk_of(ref, index):
    return jnp.concatenate([ref[2 * index : 2 * index + 1, :], ref[2 * index + 1 : 2 * index + 2, :]], axis=1)


def split(clusters, owners):
    return clusters & (owners - 1), clusters >> (owners.bit_length() - 1)


def busiest_owner(cluster_ref, owners):
    total = jnp.zeros((owners, CHUNK), jnp.float32)
    for n in range(cluster_ref.shape[0] // 2):
        owner, _ = split(chunk_of(cluster_ref, n), owners)
        total = total + jnp.where(iota((owners, CHUNK), 0) == owner, 1.0, 0.0)
    total = jnp.sum(total, axis=1, keepdims=True)
    at_top = total == jnp.max(total, axis=0, keepdims=True)
    return jnp.min(jnp.where(at_top, iota((owners, 1), 0), owners), axis=0, keepdims=True)


def owner_place_chip(clusters, owners, peers, busiest):
    owner, place = split(clusters, owners)
    ahead = (owner - busiest) & (owners - 1)
    folded = jnp.minimum(place, 2 * peers - 1 - place)
    lent = (ahead == 0) & (place >= LENT_FIRST) & (place < LENT_FIRST + LENT)
    host_chip = lax.shift_right_logical(jnp.full_like(place, HOST_CHIPS), 2 * place) & 3
    chip = jnp.where(ahead <= LENT, host_chip, folded >> 1)
    chip = jnp.where(lent, 0, jnp.where(ahead == 0, folded & 3, chip))
    owner = jnp.where(lent, (owner + place + 1 - LENT_FIRST) & (owners - 1), owner)
    return owner, place, chip


def pack_kernel(
    owners, peers, cluster_ref, order_ref, scale_hbm, bias_hbm, codes_hbm, out_ref, kept_ref,
    codes_half, codes_full, slots_full, table_vmem, table_smem, scale_ref, bias_ref, code_sems, small_sems,
):
    local_rows = codes_hbm.shape[0]
    me_wide = lax.axis_index("wide")
    me_narrow = lax.axis_index("narrow")
    pieces = code_sems.shape[0]
    tiles = codes_hbm.shape[1] // LANES
    piece = local_rows // pieces
    copies = [
        pltpu.make_async_copy(
            codes_hbm.at[pl.ds(n * piece, piece)], codes_half.at[pl.ds(n * piece, piece)], code_sems.at[n]
        )
        for n in range(pieces)
    ]
    small_copies = [
        pltpu.make_async_copy(scale_hbm, scale_ref, small_sems.at[0]),
        pltpu.make_async_copy(bias_hbm, bias_ref, small_sems.at[1]),
    ]
    for copy in copies + small_copies:
        copy.start()

    chunks = local_rows // CHUNK
    kept_ref[...] = cluster_ref[...]
    busiest = busiest_owner(cluster_ref, owners)
    places, masks, hots = [], [], []
    for n in range(chunks):
        owner, place, chip = owner_place_chip(chunk_of(cluster_ref, n), owners, peers, busiest)
        mask = iota((owners, CHUNK), 0) == jnp.where(chip == me_narrow >> 1, owner, -1)
        places.append(place)
        masks.append(mask)
        hots.append(jnp.where(mask, 1.0, 0.0))
    earlier = dot(jnp.concatenate(hots, axis=0).astype(jnp.bfloat16), strictly_before(), 1, 0)
    count = jnp.zeros((owners, 1), jnp.float32)
    spread = []
    for n in range(chunks):
        within = earlier[n * owners : (n + 1) * owners]
        rank = jnp.sum(jnp.where(masks[n], within + count, 0.0), axis=0, keepdims=True).astype(jnp.int32)
        count = count + within[:, CHUNK - 1 :] + hots[n][:, CHUNK - 1 :]
        slot = jnp.where((rank & 1) == (me_narrow & 1), rank >> 1, -1)
        key = places[n] * ORDER_SPAN + chunk_of(order_ref, n) + 1
        row = n * CHUNK + iota((1, CHUNK), 1)
        at_slot = iota((BLOCK, CHUNK), 0) == slot
        parts = [
            jnp.where(at_slot, part.astype(jnp.float32), 0.0).astype(jnp.bfloat16)
            for part in (row >> 6, row & 63, key >> 16, (key >> 8) & 255, key & 255)
        ]
        spread.append(jnp.concatenate(parts, axis=0))
    table = dot(
        jnp.concatenate(spread, axis=1), jnp.concatenate(hots, axis=1).astype(jnp.bfloat16), 1, 1
    )
    rows_at = table[:BLOCK] * 64.0 + table[BLOCK : 2 * BLOCK]
    wide = jnp.concatenate([count, jnp.zeros((owners, LANES - 1), jnp.float32)], axis=1)
    counts = jnp.concatenate([wide, jnp.zeros((LANES - owners, LANES), jnp.float32)], axis=0).T[:1, :owners]
    used = jnp.minimum((counts.astype(jnp.int32) + 1 - (me_narrow & 1)) >> 1, SLOTS)
    table_vmem[:, :owners] = jnp.concatenate(
        [rows_at.astype(jnp.int32), jnp.broadcast_to(used, (8, owners))], axis=0
    )
    table_copy = pltpu.make_async_copy(table_vmem, table_smem, small_sems.at[2])
    table_copy.start()
    over = jnp.where(jnp.max(count) > 2 * SLOTS, 1.0, 0.0)
    turn = (me_wide * BLOCK) & (LANES - 1)
    meta = []
    for n in range(2, 5):
        part = jnp.concatenate(
            [table[n * BLOCK : n * BLOCK + SLOTS + 1], jnp.zeros((LANES - BLOCK, owners), jnp.float32)], axis=0
        )
        part = jnp.concatenate([part, jnp.zeros((LANES, LANES - owners), jnp.float32)], axis=1).T
        meta.append(pltpu.roll(part[:owners], turn, 1))
    lane = iota((owners, LANES), 1)
    meta.append(jnp.where(lane < HALF, over, busiest.astype(jnp.float32)))

    slots_full[...] = jnp.zeros_like(slots_full)
    for n, copy in enumerate(copies):
        copy.wait()
        values = codes_half[n * piece : (n + 1) * piece, :].astype(jnp.float32)
        for tile in range(tiles):
            codes_full[pl.ds(n * piece * PITCH + tile, piece, stride=PITCH), :] = values[
                :, tile * LANES : (tile + 1) * LANES
            ]
    for copy in [table_copy] + small_copies:
        copy.wait()

    def four_owners(quarter, carry):
        four = [4 * quarter + n for n in range(4)]
        used = functools.reduce(jnp.maximum, [table_smem[BLOCK, owner] for owner in four])

        def four_rows(group, carry):
            for owner in four:
                for n in range(4):
                    slot = group * 4 + n
                    row = table_smem[slot, owner]
                    slots_full[pl.ds((owner * BLOCK + slot) * PITCH, TAKE), :] = (
                        codes_full[pl.ds(row * PITCH, TAKE), :] * scale_ref[row]
                        + bias_ref[row]
                    )
            return carry

        return lax.fori_loop(0, (used + 3) // 4, four_rows, carry)

    lax.fori_loop(0, owners // 4, four_owners, 0)

    pair = 2 * BLOCK
    width = tiles * LANES
    for n in range(owners // 2):
        values = [
            slots_full[pl.ds(n * pair * PITCH + tile, pair, stride=PITCH), :] for tile in range(tiles)
        ]
        squares = functools.reduce(jnp.add, [value * value for value in values])
        mean_square = jnp.sum(squares, axis=1, keepdims=True) * (1.0 / width)
        factor = lax.rsqrt(mean_square + epsilon)
        place = iota((pair, 1), 0)
        for tile in range(tiles):
            unit = values[tile] * factor
            unit = jnp.where(place == SLOTS, meta[tile][2 * n : 2 * n + 1], unit)
            unit = jnp.where(place == BLOCK + SLOTS, meta[tile][2 * n + 1 : 2 * n + 2], unit)
            out_ref[n * pair : (n + 1) * pair, tile * LANES : (tile + 1) * LANES] = unit.astype(jnp.bfloat16)


def pack(row_codes, row_scales, row_biases, cluster_ids, order_index, owners, peers):
    local_rows, width = row_codes.shape
    whole = pl.BlockSpec(memory_space=pltpu.VMEM)
    outside = pl.BlockSpec(memory_space=pl.ANY)
    pieces = 8
    return pl.pallas_call(
        functools.partial(pack_kernel, owners, peers),
        out_shape=(
            jax.ShapeDtypeStruct((owners * BLOCK, width), jnp.bfloat16),
            jax.ShapeDtypeStruct((local_rows // LANES, LANES), jnp.int32),
        ),
        in_specs=[whole, whole, outside, outside, outside],
        out_specs=(whole, whole),
        scratch_shapes=[
            pltpu.VMEM((local_rows, width), jnp.bfloat16),
            pltpu.VMEM((local_rows * PITCH + 8, LANES), jnp.float32),
            pltpu.VMEM((owners * BLOCK * PITCH + 8, LANES), jnp.float32),
            pltpu.VMEM((BLOCK + 8, LANES), jnp.int32),
            pltpu.SMEM((BLOCK + 8, LANES), jnp.int32),
            pltpu.SMEM((local_rows,), jnp.float32),
            pltpu.SMEM((local_rows,), jnp.float32),
            pltpu.SemaphoreType.DMA((pieces,)),
            pltpu.SemaphoreType.DMA((3,)),
        ],
        compiler_params=pltpu.CompilerParams(vmem_limit_bytes=VMEM_LIMIT),
        name="pack",
    )(
        cluster_ids.reshape(-1, LANES), order_index.reshape(-1, LANES), row_scales, row_biases, row_codes,
    )


def place_kernel(owners, peers, cluster_ref, group_ref, slot_ref):
    groups = owners * peers // 2
    before = strictly_before()
    count = jnp.zeros((groups, 1), jnp.float32)
    busiest = busiest_owner(cluster_ref, owners)
    for n in range(cluster_ref.shape[0] // 2):
        owner, _, chip = owner_place_chip(chunk_of(cluster_ref, n), owners, peers, busiest)
        mine = iota((groups, CHUNK), 0) == chip * owners + owner
        one_hot = jnp.where(mine, 1.0, 0.0)
        earlier = dot(one_hot.astype(jnp.bfloat16), before, 1, 0) + count
        rank = jnp.sum(jnp.where(mine, earlier, 0.0), axis=0, keepdims=True).astype(jnp.int32)
        count = count + jnp.sum(one_hot, axis=1, keepdims=True)
        peer = 2 * chip + (rank & 1)
        group = ((owner >> 3) * peers + peer) * 8 + (owner & 7)
        slot = jnp.minimum(rank >> 1, SLOTS)
        for half in range(2):
            part = slice(half * LANES, (half + 1) * LANES)
            group_ref[2 * n + half : 2 * n + half + 1, :] = group[:, part]
            slot_ref[2 * n + half : 2 * n + half + 1, :] = slot[:, part]


def places(clusters, owners, peers):
    whole = pl.BlockSpec(memory_space=pltpu.VMEM)
    shape = jax.ShapeDtypeStruct(clusters.shape, jnp.int32)
    return pl.pallas_call(
        functools.partial(place_kernel, owners, peers),
        out_shape=(shape, shape),
        in_specs=[whole],
        out_specs=(whole, whole),
        compiler_params=pltpu.CompilerParams(vmem_limit_bytes=VMEM_LIMIT),
        cost_estimate=pl.CostEstimate(flops=2**30, bytes_accessed=2**16, transcendentals=0),
        name="places",
    )(clusters)


def in_block(owners, tile, length):
    place = tile * LANES + iota((owners, LANES), 1) - iota((owners, LANES), 0) * BLOCK
    return (place >= 0) & (place < length)


def keys_of(owners, rows_ref, meta_ref):
    for n in range(owners):
        last = n * BLOCK + SLOTS
        start = last // 16 * 16
        meta_ref[n : n + 1, :] = rows_ref[start : start + 16, :].astype(jnp.float32)[last - start : last - start + 1, :]
    meta = meta_ref[...]
    key = meta[:, :LANES] * 65536.0 + meta[:, LANES : 2 * LANES] * 256.0 + meta[:, 2 * LANES : 3 * LANES]
    flat = [
        jnp.sum(jnp.where(in_block(owners, tile, SLOTS), key, 0.0), axis=0, keepdims=True)
        for tile in range(rows_ref.shape[0] // LANES)
    ]
    over = jnp.max(meta[:, 3 * LANES : 3 * LANES + HALF])
    busiest = meta[:, 3 * LANES + HALF :]
    return flat, jnp.where(jnp.max(busiest) == jnp.min(busiest), over, 1.0)


def fold(rows_ref, key_rows_ref, keys, query_ref, best_in, best_ref):
    slots, width = rows_ref.shape
    for tile in range(0, slots // LANES, 2):
        scores = dot(rows_ref[tile * LANES : (tile + 2) * LANES, :], key_rows_ref[...], 1, 1)
        mine = jnp.concatenate([query_ref[:, tile : tile + 1], query_ref[:, tile + 1 : tile + 2]], axis=0)
        first = jnp.floor((mine - 1.0) * (1.0 / ORDER_SPAN)) * ORDER_SPAN
        allowed = (keys < mine) & (keys > first)
        best = jnp.max(jnp.where(allowed, scores, -float(width)), axis=1, keepdims=True) * (1.0 / width)
        best = jnp.maximum(best, -1.0)
        for half in range(2):
            part = best[half * LANES : (half + 1) * LANES]
            if best_in is not None:
                part = jnp.maximum(part, best_in[:, tile + half : tile + half + 1])
            best_ref[:, tile + half : tile + half + 1] = part


def own_kernel(owners, rows_ref, query_ref, best_ref, meta_ref):
    flat, _ = keys_of(owners, rows_ref, meta_ref)
    query_ref[...] = jnp.concatenate(
        flat + [jnp.zeros((LANES - len(flat), LANES), jnp.float32)], axis=0
    ).T
    fold(rows_ref, rows_ref, jnp.concatenate(flat, axis=1), query_ref, None, best_ref)


def other_kernel(owners, rows_ref, other_ref, query_ref, best_in, out_ref, meta_ref, best_ref):
    flat, over = keys_of(owners, other_ref, meta_ref)
    fold(rows_ref, other_ref, jnp.concatenate(flat, axis=1), query_ref, best_in, best_ref)
    turned = best_ref[...].T
    result = jnp.zeros((owners, LANES), jnp.float32)
    for tile in range(len(flat)):
        result = jnp.where(in_block(owners, tile, SLOTS), turned[tile : tile + 1, :], result)
        result = jnp.where(in_block(owners, tile, BLOCK) & ~in_block(owners, tile, SLOTS), over, result)
    out_ref[...] = result


def score(rows, clusters, owners):
    slots, width = rows.shape
    whole = pl.BlockSpec(memory_space=pltpu.VMEM)
    square = jax.ShapeDtypeStruct((LANES, LANES), jnp.float32)
    cost = pl.CostEstimate(
        flops=2 * slots * slots * width, bytes_accessed=4 * slots * width, transcendentals=0
    )
    peers = lax.axis_size("narrow")
    other = lax.ppermute(rows, "narrow", [(n, n ^ 1) for n in range(peers)])
    meta = pltpu.VMEM((owners, width), jnp.float32)
    params = pltpu.CompilerParams(vmem_limit_bytes=VMEM_LIMIT)
    query, best = pl.pallas_call(
        functools.partial(own_kernel, owners),
        out_shape=(square, square),
        in_specs=[whole],
        out_specs=(whole, whole),
        scratch_shapes=[meta],
        compiler_params=params,
        cost_estimate=cost,
        name="score_own",
    )(rows)
    group, slot = places(clusters, owners, peers)
    other, query, best, group, slot = lax.optimization_barrier((other, query, best, group, slot))
    result = pl.pallas_call(
        functools.partial(other_kernel, owners),
        out_shape=jax.ShapeDtypeStruct((owners, LANES), jnp.float32),
        in_specs=[whole] * 4,
        out_specs=whole,
        scratch_shapes=[meta, pltpu.VMEM((LANES, LANES), jnp.float32)],
        compiler_params=params,
        cost_estimate=cost,
        name="score_other",
    )(rows, other, query, best)
    return result, group, slot


def spread_kernel(back_ref, out_ref):
    turn = (lax.axis_index("wide") * BLOCK) & (LANES - 1)
    lane = iota((8, LANES), 1) // BLOCK
    dense = jnp.zeros((8, LANES), jnp.float32)
    for n in range(LANES // BLOCK):
        part = pltpu.roll(back_ref[8 * n : 8 * n + 8, :], (n * BLOCK + LANES - turn) & (LANES - 1), 1)
        dense = jnp.where(lane == n, part, dense)
    for n in range(out_ref.shape[0]):
        out_ref[n] = dense


def spread(back, peers):
    whole = pl.BlockSpec(memory_space=pltpu.VMEM)
    return pl.pallas_call(
        spread_kernel,
        out_shape=jax.ShapeDtypeStruct((peers, 8, LANES), jnp.float32),
        in_specs=[whole],
        out_specs=whole,
        compiler_params=pltpu.CompilerParams(vmem_limit_bytes=VMEM_LIMIT),
        name="spread",
    )(back)


def pick_kernel(values_ref, group_ref, slot_ref, out_ref, over_ref):
    turned = values_ref[...].T
    values = jnp.concatenate(
        [turned[n * BLOCK : (n + 1) * BLOCK] for n in range(LANES // BLOCK)], axis=1
    )
    groups = values.shape[1]
    over_ref[0, 0] = jnp.max(values[SLOTS:]).astype(jnp.int32)
    high = values.astype(jnp.bfloat16)
    rest = values - high.astype(jnp.float32)
    middle = rest.astype(jnp.bfloat16)
    low = (rest - middle.astype(jnp.float32)).astype(jnp.bfloat16)
    parts = jnp.concatenate([high, middle, low], axis=0)
    for n in range(group_ref.shape[0] // 2):
        one_hot = jnp.where(iota((groups, CHUNK), 0) == chunk_of(group_ref, n), 1.0, 0.0).astype(jnp.bfloat16)
        by_slot = dot(parts, one_hot, 1, 0)
        by_slot = by_slot[:BLOCK] + by_slot[BLOCK : 2 * BLOCK] + by_slot[2 * BLOCK :]
        here = iota((BLOCK, CHUNK), 0) == chunk_of(slot_ref, n)
        picked = jnp.sum(jnp.where(here, by_slot, 0.0), axis=0, keepdims=True)
        out_ref[2 * n : 2 * n + 1, :] = picked[:, :LANES]
        out_ref[2 * n + 1 : 2 * n + 2, :] = picked[:, LANES:]


def pick(values, group, slot):
    whole = pl.BlockSpec(memory_space=pltpu.VMEM)
    return pl.pallas_call(
        pick_kernel,
        out_shape=(
            jax.ShapeDtypeStruct(group.shape, jnp.float32),
            jax.ShapeDtypeStruct((1, 1), jnp.int32),
        ),
        in_specs=[whole, whole, whole],
        out_specs=(whole, pl.BlockSpec(memory_space=pltpu.SMEM)),
        compiler_params=pltpu.CompilerParams(vmem_limit_bytes=VMEM_LIMIT),
        name="pick",
    )(values, group, slot)


def unit_vectors(row_codes, row_scales, row_biases):
    values = row_codes.astype(jnp.float32) * row_scales[:, None] + row_biases[:, None]
    return (values * lax.rsqrt(jnp.mean(values * values, axis=1, keepdims=True) + epsilon)).astype(
        jnp.bfloat16
    )


def fold_block(
    queries, query_cluster, query_order, running, block_rows, block_cluster, block_order
):
    feature_width = queries.shape[-1]
    scores = (
        jnp.einsum("qe,ke->qk", queries, block_rows, preferred_element_type=jnp.float32)
        / feature_width
    )
    allowed = (query_cluster[:, None] == block_cluster[None, :]) & (
        block_order[None, :] < query_order[:, None]
    )
    return jnp.maximum(running, jnp.max(jnp.where(allowed, scores, -1.0), axis=1))


def fold_keys(
    queries, query_cluster, query_order, share_rows, running, piece_rows, piece_cluster, piece_order
):
    feature_width = piece_rows.shape[2]
    blocks = piece_rows.shape[1] // share_rows

    def visit_block(block_index, best_now):
        start_col = block_index * share_rows
        block_rows = lax.dynamic_slice_in_dim(piece_rows, start_col, share_rows, 1).reshape(
            -1, feature_width
        )
        block_cluster = lax.dynamic_slice_in_dim(piece_cluster, start_col, share_rows, 1).reshape(
            -1
        )
        block_order = lax.dynamic_slice_in_dim(piece_order, start_col, share_rows, 1).reshape(-1)
        return fold_block(
            queries, query_cluster, query_order, best_now, block_rows, block_cluster, block_order
        )

    return lax.fori_loop(0, blocks, visit_block, running)


def any_skew(row_codes, row_scales, row_biases, cluster_ids, order_index):
    owners = lax.axis_size("wide")
    peer_count = lax.axis_size("narrow")
    local_rows = row_codes.shape[0]
    feature_width = row_codes.shape[1]
    capacity = 2 * local_rows // owners
    share_rows = capacity // peer_count
    total_slots = owners * capacity
    unit_rows = unit_vectors(row_codes, row_scales, row_biases)
    owner_of = cluster_ids % owners
    one_hot = (owner_of[:, None] == jnp.arange(owners, dtype=jnp.int32)[None, :]).astype(jnp.int32)
    before = jnp.cumsum(one_hot, axis=0) - one_hot
    slot_rank = jnp.sum(before * one_hot, axis=1)
    slot_index = owner_of * capacity + slot_rank
    send_rows = jnp.zeros((total_slots, feature_width), jnp.bfloat16).at[slot_index].set(unit_rows)
    send_rows = send_rows.reshape(owners, capacity, feature_width)
    send_cluster = (
        jnp.full((total_slots,), -1, jnp.int32)
        .at[slot_index]
        .set(cluster_ids)
        .reshape(owners, capacity)
    )
    send_order = (
        jnp.full((total_slots,), -1, jnp.int32)
        .at[slot_index]
        .set(order_index)
        .reshape(owners, capacity)
    )
    offset = lax.axis_index("narrow") * share_rows
    initial = jnp.full((owners * share_rows,), -1.0, jnp.float32)
    got_rows, got_cluster, got_order = (
        lax.all_to_all(send_rows, "wide", split_axis=0, concat_axis=0, tiled=True),
        lax.all_to_all(send_cluster, "wide", split_axis=0, concat_axis=0, tiled=True),
        lax.all_to_all(send_order, "wide", split_axis=0, concat_axis=0, tiled=True),
    )
    queries = lax.dynamic_slice_in_dim(got_rows, offset, share_rows, 1).reshape(-1, feature_width)
    query_cluster = lax.dynamic_slice_in_dim(got_cluster, offset, share_rows, 1).reshape(-1)
    query_order = lax.dynamic_slice_in_dim(got_order, offset, share_rows, 1).reshape(-1)
    best_sim = fold_keys(
        queries, query_cluster, query_order, share_rows, initial, got_rows, got_cluster, got_order
    )
    column = lax.all_gather(best_sim.reshape(owners, share_rows), "narrow", axis=1, tiled=True)
    returned = lax.all_to_all(column, "wide", split_axis=0, concat_axis=0, tiled=True)
    return returned.reshape(-1)[slot_index]


def shards(row_codes, row_scales, row_biases, cluster_ids, order_index):
    owners = lax.axis_size("wide")
    peers = lax.axis_size("narrow")
    width = row_codes.shape[1]
    sent, clusters = pack(row_codes, row_scales, row_biases, cluster_ids, order_index, owners, peers)
    got = lax.all_to_all(
        sent.reshape(owners, BLOCK, width), "wide", split_axis=0, concat_axis=0, tiled=True
    ).reshape(owners * BLOCK, width)
    best, group, slot = score(got, clusters, owners)
    back = lax.all_to_all(best.reshape(owners, 1, LANES), "wide", split_axis=0, concat_axis=0, tiled=True)
    copies = spread(back.reshape(owners, LANES), peers)
    values = lax.all_to_all(copies, "narrow", split_axis=0, concat_axis=0, tiled=True)
    values = values.reshape(peers * 8, LANES)
    picked, over = pick(values, group, slot)
    _, result = lax.while_loop(
        lambda state: state[0] > 0,
        lambda state: (
            jnp.zeros_like(state[0]),
            any_skew(row_codes, row_scales, row_biases, cluster_ids, order_index),
        ),
        (over[0, 0], picked.reshape(-1)),
    )
    return result


def solution(mesh):
    in_specs = (P("wide", None), P("wide"), P("wide"), P("wide"), P("wide"))
    out_specs = P("wide")
    return jax.shard_map(shards, mesh=mesh, in_specs=in_specs, out_specs=out_specs, check_vma=False)
```

```python
import functools

import jax
import jax.numpy as jnp
from jax import lax
from jax.experimental import pallas as pl
from jax.experimental.pallas import tpu as pltpu
from jax.sharding import PartitionSpec as P

epsilon = 1e-06

BLOCK = 32
SLOTS = BLOCK - 1
LANES = 128
HALF = LANES // 2
PITCH = 5
LENT_FIRST, LENT = 4, 8
HOST_CHIPS = -1620452551
TAKE = 4
CHUNK = 256
ORDER_SPAN = 131072
VMEM_LIMIT = 48 * 1024 * 1024


def iota(shape, axis):
    return lax.broadcasted_iota(jnp.int32, shape, axis)


def dot(left, right, left_axis, right_axis):
    return lax.dot_general(
        left, right, (((left_axis,), (right_axis,)), ((), ())), preferred_element_type=jnp.float32
    )


def strictly_before():
    return (iota((CHUNK, CHUNK), 0) < iota((CHUNK, CHUNK), 1)).astype(jnp.bfloat16)


def chunk_of(ref, index):
    return jnp.concatenate([ref[2 * index : 2 * index + 1, :], ref[2 * index + 1 : 2 * index + 2, :]], axis=1)


def split(clusters, owners):
    return clusters & (owners - 1), clusters >> (owners.bit_length() - 1)


def busiest_owner(cluster_ref, owners):
    total = jnp.zeros((owners, CHUNK), jnp.float32)
    for n in range(cluster_ref.shape[0] // 2):
        owner, _ = split(chunk_of(cluster_ref, n), owners)
        total = total + jnp.where(iota((owners, CHUNK), 0) == owner, 1.0, 0.0)
    total = jnp.sum(total, axis=1, keepdims=True)
    at_top = total == jnp.max(total, axis=0, keepdims=True)
    return jnp.min(jnp.where(at_top, iota((owners, 1), 0), owners), axis=0, keepdims=True)


def owner_place_chip(clusters, owners, peers, busiest):
    owner, place = split(clusters, owners)
    ahead = (owner - busiest) & (owners - 1)
    folded = jnp.minimum(place, 2 * peers - 1 - place)
    lent = (ahead == 0) & (place >= LENT_FIRST) & (place < LENT_FIRST + LENT)
    host_chip = lax.shift_right_logical(jnp.full_like(place, HOST_CHIPS), 2 * place) & 3
    chip = jnp.where(ahead <= LENT, host_chip, folded >> 1)
    chip = jnp.where(lent, 0, jnp.where(ahead == 0, folded & 3, chip))
    owner = jnp.where(lent, (owner + place + 1 - LENT_FIRST) & (owners - 1), owner)
    return owner, place, chip


def pack_kernel(
    owners, peers, cluster_ref, order_ref, scale_hbm, bias_hbm, codes_hbm, out_ref, kept_ref,
    codes_half, codes_full, slots_full, table_vmem, table_smem, scale_ref, bias_ref, code_sems, small_sems,
):
    local_rows = codes_hbm.shape[0]
    me_wide = lax.axis_index("wide")
    me_narrow = lax.axis_index("narrow")
    pieces = code_sems.shape[0]
    tiles = codes_hbm.shape[1] // LANES
    piece = local_rows // pieces
    copies = [
        pltpu.make_async_copy(
            codes_hbm.at[pl.ds(n * piece, piece)], codes_half.at[pl.ds(n * piece, piece)], code_sems.at[n]
        )
        for n in range(pieces)
    ]
    small_copies = [
        pltpu.make_async_copy(scale_hbm, scale_ref, small_sems.at[0]),
        pltpu.make_async_copy(bias_hbm, bias_ref, small_sems.at[1]),
    ]
    for copy in copies + small_copies:
        copy.start()

    chunks = local_rows // CHUNK
    kept_ref[...] = cluster_ref[...]
    busiest = busiest_owner(cluster_ref, owners)
    places, masks, hots = [], [], []
    for n in range(chunks):
        owner, place, chip = owner_place_chip(chunk_of(cluster_ref, n), owners, peers, busiest)
        mask = iota((owners, CHUNK), 0) == jnp.where(chip == me_narrow >> 1, owner, -1)
        places.append(place)
        masks.append(mask)
        hots.append(jnp.where(mask, 1.0, 0.0))
    earlier = dot(jnp.concatenate(hots, axis=0).astype(jnp.bfloat16), strictly_before(), 1, 0)
    count = jnp.zeros((owners, 1), jnp.float32)
    spread = []
    for n in range(chunks):
        within = earlier[n * owners : (n + 1) * owners]
        rank = jnp.sum(jnp.where(masks[n], within + count, 0.0), axis=0, keepdims=True).astype(jnp.int32)
        count = count + within[:, CHUNK - 1 :] + hots[n][:, CHUNK - 1 :]
        slot = jnp.where((rank & 1) == (me_narrow & 1), rank >> 1, -1)
        key = places[n] * ORDER_SPAN + chunk_of(order_ref, n) + 1
        row = n * CHUNK + iota((1, CHUNK), 1)
        at_slot = iota((BLOCK, CHUNK), 0) == slot
        parts = [
            jnp.where(at_slot, part.astype(jnp.float32), 0.0).astype(jnp.bfloat16)
            for part in (row >> 6, row & 63, key >> 16, (key >> 8) & 255, key & 255)
        ]
        spread.append(jnp.concatenate(parts, axis=0))
    table = dot(
        jnp.concatenate(spread, axis=1), jnp.concatenate(hots, axis=1).astype(jnp.bfloat16), 1, 1
    )
    rows_at = table[:BLOCK] * 64.0 + table[BLOCK : 2 * BLOCK]
    wide = jnp.concatenate([count, jnp.zeros((owners, LANES - 1), jnp.float32)], axis=1)
    counts = jnp.concatenate([wide, jnp.zeros((LANES - owners, LANES), jnp.float32)], axis=0).T[:1, :owners]
    used = jnp.minimum((counts.astype(jnp.int32) + 1 - (me_narrow & 1)) >> 1, SLOTS)
    table_vmem[:, :owners] = jnp.concatenate(
        [rows_at.astype(jnp.int32), jnp.broadcast_to(used, (8, owners))], axis=0
    )
    table_copy = pltpu.make_async_copy(table_vmem, table_smem, small_sems.at[2])
    table_copy.start()
    over = jnp.where(jnp.max(count) > 2 * SLOTS, 1.0, 0.0)
    turn = (me_wide * BLOCK) & (LANES - 1)
    meta = []
    for n in range(2, 5):
        part = jnp.concatenate(
            [table[n * BLOCK : n * BLOCK + SLOTS + 1], jnp.zeros((LANES - BLOCK, owners), jnp.float32)], axis=0
        )
        part = jnp.concatenate([part, jnp.zeros((LANES, LANES - owners), jnp.float32)], axis=1).T
        meta.append(pltpu.roll(part[:owners], turn, 1))
    lane = iota((owners, LANES), 1)
    meta.append(jnp.where(lane < HALF, over, busiest.astype(jnp.float32)))

    slots_full[...] = jnp.zeros_like(slots_full)
    for n, copy in enumerate(copies):
        copy.wait()
        values = codes_half[n * piece : (n + 1) * piece, :].astype(jnp.float32)
        for tile in range(tiles):
            codes_full[pl.ds(n * piece * PITCH + tile, piece, stride=PITCH), :] = values[
                :, tile * LANES : (tile + 1) * LANES
            ]
    for copy in [table_copy] + small_copies:
        copy.wait()

    def four_owners(quarter, carry):
        four = [4 * quarter + n for n in range(4)]
        used = functools.reduce(jnp.maximum, [table_smem[BLOCK, owner] for owner in four])

        def four_rows(group, carry):
            for owner in four:
                for n in range(4):
                    slot = group * 4 + n
                    row = table_smem[slot, owner]
                    slots_full[pl.ds((owner * BLOCK + slot) * PITCH, TAKE), :] = (
                        codes_full[pl.ds(row * PITCH, TAKE), :] * scale_ref[row]
                        + bias_ref[row]
                    )
            return carry

        return lax.fori_loop(0, (used + 3) // 4, four_rows, carry)

    lax.fori_loop(0, owners // 4, four_owners, 0)

    pair = 2 * BLOCK
    width = tiles * LANES
    for n in range(owners // 2):
        values = [
            slots_full[pl.ds(n * pair * PITCH + tile, pair, stride=PITCH), :] for tile in range(tiles)
        ]
        squares = functools.reduce(jnp.add, [value * value for value in values])
        mean_square = jnp.sum(squares, axis=1, keepdims=True) * (1.0 / width)
        factor = lax.rsqrt(mean_square + epsilon)
        place = iota((pair, 1), 0)
        for tile in range(tiles):
            unit = values[tile] * factor
            unit = jnp.where(place == SLOTS, meta[tile][2 * n : 2 * n + 1], unit)
            unit = jnp.where(place == BLOCK + SLOTS, meta[tile][2 * n + 1 : 2 * n + 2], unit)
            out_ref[n * pair : (n + 1) * pair, tile * LANES : (tile + 1) * LANES] = unit.astype(jnp.bfloat16)


def pack(row_codes, row_scales, row_biases, cluster_ids, order_index, owners, peers):
    local_rows, width = row_codes.shape
    whole = pl.BlockSpec(memory_space=pltpu.VMEM)
    outside = pl.BlockSpec(memory_space=pl.ANY)
    pieces = 8
    return pl.pallas_call(
        functools.partial(pack_kernel, owners, peers),
        out_shape=(
            jax.ShapeDtypeStruct((owners * BLOCK, width), jnp.bfloat16),
            jax.ShapeDtypeStruct((local_rows // LANES, LANES), jnp.int32),
        ),
        in_specs=[whole, whole, outside, outside, outside],
        out_specs=(whole, whole),
        scratch_shapes=[
            pltpu.VMEM((local_rows, width), jnp.bfloat16),
            pltpu.VMEM((local_rows * PITCH + 8, LANES), jnp.float32),
            pltpu.VMEM((owners * BLOCK * PITCH + 8, LANES), jnp.float32),
            pltpu.VMEM((BLOCK + 8, LANES), jnp.int32),
            pltpu.SMEM((BLOCK + 8, LANES), jnp.int32),
            pltpu.SMEM((local_rows,), jnp.float32),
            pltpu.SMEM((local_rows,), jnp.float32),
            pltpu.SemaphoreType.DMA((pieces,)),
            pltpu.SemaphoreType.DMA((3,)),
        ],
        compiler_params=pltpu.CompilerParams(vmem_limit_bytes=VMEM_LIMIT),
        name="pack",
    )(
        cluster_ids.reshape(-1, LANES), order_index.reshape(-1, LANES), row_scales, row_biases, row_codes,
    )


def place_kernel(owners, peers, cluster_ref, group_ref, slot_ref):
    groups = owners * peers // 2
    before = strictly_before()
    count = jnp.zeros((groups, 1), jnp.float32)
    busiest = busiest_owner(cluster_ref, owners)
    for n in range(cluster_ref.shape[0] // 2):
        owner, _, chip = owner_place_chip(chunk_of(cluster_ref, n), owners, peers, busiest)
        mine = iota((groups, CHUNK), 0) == chip * owners + owner
        one_hot = jnp.where(mine, 1.0, 0.0)
        earlier = dot(one_hot.astype(jnp.bfloat16), before, 1, 0) + count
        rank = jnp.sum(jnp.where(mine, earlier, 0.0), axis=0, keepdims=True).astype(jnp.int32)
        count = count + jnp.sum(one_hot, axis=1, keepdims=True)
        peer = 2 * chip + (rank & 1)
        group = ((owner >> 3) * peers + peer) * 8 + (owner & 7)
        slot = jnp.minimum(rank >> 1, SLOTS)
        for half in range(2):
            part = slice(half * LANES, (half + 1) * LANES)
            group_ref[2 * n + half : 2 * n + half + 1, :] = group[:, part]
            slot_ref[2 * n + half : 2 * n + half + 1, :] = slot[:, part]


def places(clusters, owners, peers):
    whole = pl.BlockSpec(memory_space=pltpu.VMEM)
    shape = jax.ShapeDtypeStruct(clusters.shape, jnp.int32)
    return pl.pallas_call(
        functools.partial(place_kernel, owners, peers),
        out_shape=(shape, shape),
        in_specs=[whole],
        out_specs=(whole, whole),
        compiler_params=pltpu.CompilerParams(vmem_limit_bytes=VMEM_LIMIT),
        cost_estimate=pl.CostEstimate(flops=2**30, bytes_accessed=2**16, transcendentals=0),
        name="places",
    )(clusters)


def in_block(owners, tile, length):
    place = tile * LANES + iota((owners, LANES), 1) - iota((owners, LANES), 0) * BLOCK
    return (place >= 0) & (place < length)


def keys_of(owners, rows_ref, meta_ref):
    for n in range(owners):
        last = n * BLOCK + SLOTS
        start = last // 16 * 16
        meta_ref[n : n + 1, :] = rows_ref[start : start + 16, :].astype(jnp.float32)[last - start : last - start + 1, :]
    meta = meta_ref[...]
    key = meta[:, :LANES] * 65536.0 + meta[:, LANES : 2 * LANES] * 256.0 + meta[:, 2 * LANES : 3 * LANES]
    flat = [
        jnp.sum(jnp.where(in_block(owners, tile, SLOTS), key, 0.0), axis=0, keepdims=True)
        for tile in range(rows_ref.shape[0] // LANES)
    ]
    over = jnp.max(meta[:, 3 * LANES : 3 * LANES + HALF])
    busiest = meta[:, 3 * LANES + HALF :]
    return flat, jnp.where(jnp.max(busiest) == jnp.min(busiest), over, 1.0)


def fold(rows_ref, key_rows_ref, keys, query_ref, best_in, best_ref):
    slots, width = rows_ref.shape
    for tile in range(0, slots // LANES, 2):
        scores = dot(rows_ref[tile * LANES : (tile + 2) * LANES, :], key_rows_ref[...], 1, 1)
        mine = jnp.concatenate([query_ref[:, tile : tile + 1], query_ref[:, tile + 1 : tile + 2]], axis=0)
        first = jnp.floor((mine - 1.0) * (1.0 / ORDER_SPAN)) * ORDER_SPAN
        allowed = (keys < mine) & (keys > first)
        best = jnp.max(jnp.where(allowed, scores, -float(width)), axis=1, keepdims=True) * (1.0 / width)
        best = jnp.maximum(best, -1.0)
        for half in range(2):
            part = best[half * LANES : (half + 1) * LANES]
            if best_in is not None:
                part = jnp.maximum(part, best_in[:, tile + half : tile + half + 1])
            best_ref[:, tile + half : tile + half + 1] = part


def own_kernel(owners, rows_ref, query_ref, best_ref, meta_ref):
    flat, _ = keys_of(owners, rows_ref, meta_ref)
    query_ref[...] = jnp.concatenate(
        flat + [jnp.zeros((LANES - len(flat), LANES), jnp.float32)], axis=0
    ).T
    fold(rows_ref, rows_ref, jnp.concatenate(flat, axis=1), query_ref, None, best_ref)


def other_kernel(owners, rows_ref, other_ref, query_ref, best_in, out_ref, meta_ref, best_ref):
    flat, over = keys_of(owners, other_ref, meta_ref)
    fold(rows_ref, other_ref, jnp.concatenate(flat, axis=1), query_ref, best_in, best_ref)
    turned = best_ref[...].T
    result = jnp.zeros((owners, LANES), jnp.float32)
    for tile in range(len(flat)):
        result = jnp.where(in_block(owners, tile, SLOTS), turned[tile : tile + 1, :], result)
        result = jnp.where(in_block(owners, tile, BLOCK) & ~in_block(owners, tile, SLOTS), over, result)
    out_ref[...] = result


def score(rows, clusters, owners):
    slots, width = rows.shape
    whole = pl.BlockSpec(memory_space=pltpu.VMEM)
    square = jax.ShapeDtypeStruct((LANES, LANES), jnp.float32)
    cost = pl.CostEstimate(
        flops=2 * slots * slots * width, bytes_accessed=4 * slots * width, transcendentals=0
    )
    peers = lax.axis_size("narrow")
    other = lax.ppermute(rows, "narrow", [(n, n ^ 1) for n in range(peers)])
    meta = pltpu.VMEM((owners, width), jnp.float32)
    params = pltpu.CompilerParams(vmem_limit_bytes=VMEM_LIMIT)
    query, best = pl.pallas_call(
        functools.partial(own_kernel, owners),
        out_shape=(square, square),
        in_specs=[whole],
        out_specs=(whole, whole),
        scratch_shapes=[meta],
        compiler_params=params,
        cost_estimate=cost,
        name="score_own",
    )(rows)
    group, slot = places(clusters, owners, peers)
    other, query, best, group, slot = lax.optimization_barrier((other, query, best, group, slot))
    result = pl.pallas_call(
        functools.partial(other_kernel, owners),
        out_shape=jax.ShapeDtypeStruct((owners, LANES), jnp.float32),
        in_specs=[whole] * 4,
        out_specs=whole,
        scratch_shapes=[meta, pltpu.VMEM((LANES, LANES), jnp.float32)],
        compiler_params=params,
        cost_estimate=cost,
        name="score_other",
    )(rows, other, query, best)
    return result, group, slot


def spread_kernel(back_ref, out_ref):
    turn = (lax.axis_index("wide") * BLOCK) & (LANES - 1)
    lane = iota((8, LANES), 1) // BLOCK
    dense = jnp.zeros((8, LANES), jnp.float32)
    for n in range(LANES // BLOCK):
        part = pltpu.roll(back_ref[8 * n : 8 * n + 8, :], (n * BLOCK + LANES - turn) & (LANES - 1), 1)
        dense = jnp.where(lane == n, part, dense)
    for n in range(out_ref.shape[0]):
        out_ref[n] = dense


def spread(back, peers):
    whole = pl.BlockSpec(memory_space=pltpu.VMEM)
    return pl.pallas_call(
        spread_kernel,
        out_shape=jax.ShapeDtypeStruct((peers, 8, LANES), jnp.float32),
        in_specs=[whole],
        out_specs=whole,
        compiler_params=pltpu.CompilerParams(vmem_limit_bytes=VMEM_LIMIT),
        name="spread",
    )(back)


def pick_kernel(values_ref, group_ref, slot_ref, out_ref, over_ref):
    turned = values_ref[...].T
    values = jnp.concatenate(
        [turned[n * BLOCK : (n + 1) * BLOCK] for n in range(LANES // BLOCK)], axis=1
    )
    groups = values.shape[1]
    over_ref[0, 0] = jnp.max(values[SLOTS:]).astype(jnp.int32)
    high = values.astype(jnp.bfloat16)
    rest = values - high.astype(jnp.float32)
    middle = rest.astype(jnp.bfloat16)
    low = (rest - middle.astype(jnp.float32)).astype(jnp.bfloat16)
    parts = jnp.concatenate([high, middle, low], axis=0)
    chunks = group_ref.shape[0] // 2
    hots = [
        jnp.where(iota((groups, CHUNK), 0) == chunk_of(group_ref, n), 1.0, 0.0).astype(jnp.bfloat16)
        for n in range(chunks)
    ]
    by_slot = dot(parts, jnp.concatenate(hots, axis=1), 1, 0)
    by_slot = by_slot[:BLOCK] + by_slot[BLOCK : 2 * BLOCK] + by_slot[2 * BLOCK :]
    for n in range(chunks):
        here = iota((BLOCK, CHUNK), 0) == chunk_of(slot_ref, n)
        mine = by_slot[:, n * CHUNK : (n + 1) * CHUNK]
        picked = jnp.sum(jnp.where(here, mine, 0.0), axis=0, keepdims=True)
        out_ref[2 * n : 2 * n + 1, :] = picked[:, :LANES]
        out_ref[2 * n + 1 : 2 * n + 2, :] = picked[:, LANES:]


def pick(values, group, slot):
    whole = pl.BlockSpec(memory_space=pltpu.VMEM)
    return pl.pallas_call(
        pick_kernel,
        out_shape=(
            jax.ShapeDtypeStruct(group.shape, jnp.float32),
            jax.ShapeDtypeStruct((1, 1), jnp.int32),
        ),
        in_specs=[whole, whole, whole],
        out_specs=(whole, pl.BlockSpec(memory_space=pltpu.SMEM)),
        compiler_params=pltpu.CompilerParams(vmem_limit_bytes=VMEM_LIMIT),
        name="pick",
    )(values, group, slot)


def unit_vectors(row_codes, row_scales, row_biases):
    values = row_codes.astype(jnp.float32) * row_scales[:, None] + row_biases[:, None]
    return (values * lax.rsqrt(jnp.mean(values * values, axis=1, keepdims=True) + epsilon)).astype(
        jnp.bfloat16
    )


def fold_block(
    queries, query_cluster, query_order, running, block_rows, block_cluster, block_order
):
    feature_width = queries.shape[-1]
    scores = (
        jnp.einsum("qe,ke->qk", queries, block_rows, preferred_element_type=jnp.float32)
        / feature_width
    )
    allowed = (query_cluster[:, None] == block_cluster[None, :]) & (
        block_order[None, :] < query_order[:, None]
    )
    return jnp.maximum(running, jnp.max(jnp.where(allowed, scores, -1.0), axis=1))


def fold_keys(
    queries, query_cluster, query_order, share_rows, running, piece_rows, piece_cluster, piece_order
):
    feature_width = piece_rows.shape[2]
    blocks = piece_rows.shape[1] // share_rows

    def visit_block(block_index, best_now):
        start_col = block_index * share_rows
        block_rows = lax.dynamic_slice_in_dim(piece_rows, start_col, share_rows, 1).reshape(
            -1, feature_width
        )
        block_cluster = lax.dynamic_slice_in_dim(piece_cluster, start_col, share_rows, 1).reshape(
            -1
        )
        block_order = lax.dynamic_slice_in_dim(piece_order, start_col, share_rows, 1).reshape(-1)
        return fold_block(
            queries, query_cluster, query_order, best_now, block_rows, block_cluster, block_order
        )

    return lax.fori_loop(0, blocks, visit_block, running)


def any_skew(row_codes, row_scales, row_biases, cluster_ids, order_index):
    owners = lax.axis_size("wide")
    peer_count = lax.axis_size("narrow")
    local_rows = row_codes.shape[0]
    feature_width = row_codes.shape[1]
    capacity = 2 * local_rows // owners
    share_rows = capacity // peer_count
    total_slots = owners * capacity
    unit_rows = unit_vectors(row_codes, row_scales, row_biases)
    owner_of = cluster_ids % owners
    one_hot = (owner_of[:, None] == jnp.arange(owners, dtype=jnp.int32)[None, :]).astype(jnp.int32)
    before = jnp.cumsum(one_hot, axis=0) - one_hot
    slot_rank = jnp.sum(before * one_hot, axis=1)
    slot_index = owner_of * capacity + slot_rank
    send_rows = jnp.zeros((total_slots, feature_width), jnp.bfloat16).at[slot_index].set(unit_rows)
    send_rows = send_rows.reshape(owners, capacity, feature_width)
    send_cluster = (
        jnp.full((total_slots,), -1, jnp.int32)
        .at[slot_index]
        .set(cluster_ids)
        .reshape(owners, capacity)
    )
    send_order = (
        jnp.full((total_slots,), -1, jnp.int32)
        .at[slot_index]
        .set(order_index)
        .reshape(owners, capacity)
    )
    offset = lax.axis_index("narrow") * share_rows
    initial = jnp.full((owners * share_rows,), -1.0, jnp.float32)
    got_rows, got_cluster, got_order = (
        lax.all_to_all(send_rows, "wide", split_axis=0, concat_axis=0, tiled=True),
        lax.all_to_all(send_cluster, "wide", split_axis=0, concat_axis=0, tiled=True),
        lax.all_to_all(send_order, "wide", split_axis=0, concat_axis=0, tiled=True),
    )
    queries = lax.dynamic_slice_in_dim(got_rows, offset, share_rows, 1).reshape(-1, feature_width)
    query_cluster = lax.dynamic_slice_in_dim(got_cluster, offset, share_rows, 1).reshape(-1)
    query_order = lax.dynamic_slice_in_dim(got_order, offset, share_rows, 1).reshape(-1)
    best_sim = fold_keys(
        queries, query_cluster, query_order, share_rows, initial, got_rows, got_cluster, got_order
    )
    column = lax.all_gather(best_sim.reshape(owners, share_rows), "narrow", axis=1, tiled=True)
    returned = lax.all_to_all(column, "wide", split_axis=0, concat_axis=0, tiled=True)
    return returned.reshape(-1)[slot_index]


def shards(row_codes, row_scales, row_biases, cluster_ids, order_index):
    owners = lax.axis_size("wide")
    peers = lax.axis_size("narrow")
    width = row_codes.shape[1]
    sent, clusters = pack(row_codes, row_scales, row_biases, cluster_ids, order_index, owners, peers)
    got = lax.all_to_all(
        sent.reshape(owners, BLOCK, width), "wide", split_axis=0, concat_axis=0, tiled=True
    ).reshape(owners * BLOCK, width)
    best, group, slot = score(got, clusters, owners)
    back = lax.all_to_all(best.reshape(owners, 1, LANES), "wide", split_axis=0, concat_axis=0, tiled=True)
    copies = spread(back.reshape(owners, LANES), peers)
    values = lax.all_to_all(copies, "narrow", split_axis=0, concat_axis=0, tiled=True)
    values = values.reshape(peers * 8, LANES)
    picked, over = pick(values, group, slot)
    _, result = lax.while_loop(
        lambda state: state[0] > 0,
        lambda state: (
            jnp.zeros_like(state[0]),
            any_skew(row_codes, row_scales, row_biases, cluster_ids, order_index),
        ),
        (over[0, 0], picked.reshape(-1)),
    )
    return result


def solution(mesh):
    in_specs = (P("wide", None), P("wide"), P("wide"), P("wide"), P("wide"))
    out_specs = P("wide")
    return jax.shard_map(shards, mesh=mesh, in_specs=in_specs, out_specs=out_specs, check_vma=False)
```
